256 devices in a mesh: seq: 2 (over x_hi), head: 2 (over core), dp: 64 (over z, y, x_lo).
Axes of the slice: x: 4 (x_hi: 2, x_lo: 2; x = x_hi * 2 + x_lo), y: 4, z: 8, core: 2. Of those that a mesh axis runs over, the one named last changes fastest.
Arguments:
- tokens: bfloat16 [64, 1024, 1536], P('dp', 'seq', 'head'), may hold values from -40 to 40
- lengths: int32 [64, 8], P('dp'), may hold values from 1 to 512, 1024 in all within a row
- owner_slot: int32 [64, 8], P('dp'), may hold values from 0 to 7, each once within a row
- latent_index: int32 [64, 8, 128], P('dp'), may hold values from 0 to 1048575
- cotangent: bfloat16 [64, 1024, 1536], P('dp', 'seq'), may hold values from -24 to 24
- qkv_weight: bfloat16 [3, 1536, 1536], P(None, None, 'head'), may hold values from -0.15625 to 0.15625
- out_weight: bfloat16 [1536, 1536], P('head'), may hold values from -1.25 to 1.25
Outputs:
- mixed: bfloat16 [64, 1024, 1536], P('dp', 'seq', 'head')
- latents: bfloat16 [64, 1024, 1536], P('dp', 'seq', 'head')
- grad_out: float32 [1536, 1536], P('head')
The draws below stay inside these ranges and needn't reach their ends.
Inputs may be any that keep to these rules, and one draw needn't show every extreme that they name: Each pack's lengths sum to 1024.
All inputs are finite; a program needn't handle non-finite values.
Results may differ from the reference program's by a relative error of at most 0.013.
Values may be sent and summed in bfloat16 or wider, within the bound.
No kernel may reach another device: no remote copies, remote signals or barrier semaphores. Data moves between devices by JAX's collectives and lax.ppermute only.
A program may use at most 128 MiB of HBM per device.

```python
import math
import jax
import jax.numpy as jnp
import numpy as np
from jax import lax

D = 1536
HEADS = 24
HD = 64
LAT = 128
TOK_DEV = 512
S = 1024
IMAGES = 8
PACKS = 64


def draw_tokens(key, part):
    first, second, third = jax.random.split(key, 3)
    shape = (PACKS, S, D)
    row_scale = jnp.exp(jax.random.uniform(second, (PACKS, S, 1), jnp.float32, 0.0, 2.302585))
    col_scale = jnp.exp(jax.random.uniform(third, (1, 1, D), jnp.float32, 0.0, 2.302585))
    base = jnp.clip(jax.random.normal(first, shape, jnp.float32), -4.0, 4.0)
    return jnp.clip(base * row_scale * col_scale * 0.1, -40.0, 40.0).astype(jnp.bfloat16)


def with_ends(drawn, stream_key, least, largest):
    dims = drawn.shape
    place = [jax.random.randint(jax.random.fold_in(stream_key, axis), (), 0, dims[axis]) for axis in range(len(dims))]
    drawn = drawn.at[tuple(place)].set(least)
    longest = dims.index(max(dims))
    place[longest] = (place[longest] + 1) % dims[longest]
    return drawn.at[tuple(place)].set(largest)


def levels(rng, shape, cuts, smallest, largest):
    factor_of = 1.0
    for axis_at, blocks in cuts:
        steps = jax.random.uniform(jax.random.fold_in(jax.random.fold_in(rng, 6), axis_at), (blocks,), jnp.float32, smallest / len(cuts), largest / len(cuts))
        factor_of = factor_of * jnp.repeat(jnp.exp(steps), shape[axis_at] // blocks).reshape((-1,) + (1,) * (len(shape) - 1 - axis_at))
    return factor_of


def profile(count, total, limit, slope):
    portions = [(1 << 20) // math.isqrt(rank ** slope) + 1 for rank in range(2, count + 1)]
    spare, given = total - limit - (count - 1), [1] * (count - 1)
    while spare > 0:
        free = [i for i in range(count - 1) if given[i] < limit]
        pool, left = sum([portions[i] for i in free]), spare
        for i in free:
            addition = min(limit - given[i], max(1, left * portions[i] // pool), spare)
            given[i] = given[i] + addition
            spare = spare - addition
    return np.array([limit] + given)


def ragged(rng, count, total, most, skew):
    if count == 2:
        one = jax.random.randint(rng, (), max(1, total - most), min(most, total - 1) + 1)
        return jnp.stack([one, total - one])
    tallies = jnp.asarray(profile(count, total, most, skew), jnp.int32)
    twos = (count - 1) // 2
    donor, sink = tallies[1:1 + 2 * twos:2], tallies[2:2 + 2 * twos:2]
    room = jnp.minimum(donor - 1, most - sink)
    shifted = jax.random.randint(jax.random.fold_in(rng, 1), (twos,), 0, 1 << 20) % (room + 1)
    tallies = tallies.at[1:1 + 2 * twos:2].set(donor - shifted).at[2:2 + 2 * twos:2].set(sink + shifted)
    return tallies[jax.random.permutation(jax.random.fold_in(rng, 2), count)]


def gaussian(key, dims, spread, limit, pieces=(), kind=jnp.bfloat16):
    drawn = spread * jax.random.normal(key, dims, jnp.float32)
    if pieces:
        drawn = drawn * levels(key, dims, pieces, -0.22, 0.18)
    return jnp.clip(drawn, -limit, limit).astype(kind)


def setup_inputs(seed: int = 0) -> dict:
    key_of = jax.random.split(jax.random.key(seed), 8)
    return {
        "tokens": draw_tokens(jax.random.fold_in(key_of[7], 71), 0),
        "lengths": jax.vmap(lambda own: ragged(own, IMAGES, S, TOK_DEV, 2))(jax.random.split(key_of[1], PACKS)).reshape((PACKS, IMAGES)).astype(jnp.int32),
        "owner_slot": jax.vmap(lambda own: jax.random.permutation(own, IMAGES))(jax.random.split(key_of[2], PACKS)).reshape((PACKS, IMAGES)).astype(jnp.int32),
        "latent_index": with_ends(jax.random.randint(key_of[3], (PACKS, IMAGES, LAT), 0, 1048576), jax.random.fold_in(key_of[3], 1), 0, 1048575).astype(jnp.int32),
        "cotangent": gaussian(key_of[4], (PACKS, S, D), 4.0, 24.0, ((0, 64), (1, 2))),
        "qkv_weight": gaussian(key_of[5], (3, D, D), D ** -0.5, 0.15625, ((2, 2),)),
        "out_weight": gaussian(key_of[6], (D, D), (D // 64) ** -0.5, 1.25, ((0, 2),)),
    }


eps_norm = 1e-05
eps_head = 1e-06

def image_of(positions, ends):
    return lax.optimization_barrier(jnp.sum((positions[:, None] >= ends[None, :]).astype(jnp.int32), axis=1)).astype(jnp.int32)

def head_norm(values):
    split = values.reshape(values.shape[0], HEADS, HD)
    scale = lax.rsqrt(lax.optimization_barrier(jnp.mean(split * split, axis=2, keepdims=True)) + eps_head)
    return (split * scale).reshape(values.shape[0], D).astype(jnp.bfloat16)

def attend_pack(query, keys, values, image):
    pad_keys = jnp.pad(keys, ((TOK_DEV, TOK_DEV), (0, 0)))
    pad_values = jnp.pad(values, ((TOK_DEV, TOK_DEV), (0, 0)))
    pad_image = jnp.pad(image, (TOK_DEV, TOK_DEV), constant_values=-1)
    block = min(TOK_DEV, 512)
    window = block + 2 * TOK_DEV

    def one_block(index):
        begin = index * block
        q_blk = lax.dynamic_slice_in_dim(query, begin, block, 0).reshape(block, HEADS, HD).astype(jnp.float32)
        img_q = lax.dynamic_slice_in_dim(image, begin, block, 0)
        k_win = lax.dynamic_slice_in_dim(pad_keys, begin, window, 0).reshape(window, HEADS, HD).astype(jnp.float32)
        v_win = lax.dynamic_slice_in_dim(pad_values, begin, window, 0).reshape(window, HEADS, HD).astype(jnp.float32)
        img_k = lax.dynamic_slice_in_dim(pad_image, begin, window, 0)
        scores = jnp.einsum('qhd,khd->hqk', q_blk, k_win) * HD ** (-0.5)
        same = (img_q[:, None] == img_k[None, :]).astype(jnp.float32)
        weights = jnp.exp(scores) * same[None]
        denom = lax.optimization_barrier(jnp.sum(weights, axis=2))
        rounded = lax.optimization_barrier(weights.astype(jnp.bfloat16)).astype(jnp.float32)
        summed = jnp.einsum('hqk,khd->qhd', rounded, v_win)
        return (summed / jnp.transpose(denom)[:, :, None]).reshape(block, D).astype(jnp.bfloat16)
    out = lax.map(one_block, jnp.arange(S // block, dtype=jnp.int32))
    return out.reshape(S, D)

def one_pack(tokens, lengths, owner_slot, latent_index, cotangent, qkv_weight, out_weight):
    ends = jnp.cumsum(lengths, dtype=jnp.int32)
    starts = (ends - lengths).astype(jnp.int32)
    image = image_of(jnp.arange(S, dtype=jnp.int32), ends)
    rows = tokens.astype(jnp.float32)
    mean = lax.optimization_barrier(jnp.mean(rows, axis=1, keepdims=True))
    centered = rows - mean
    var = lax.optimization_barrier(jnp.mean(centered * centered, axis=1, keepdims=True))
    normed = (centered * lax.rsqrt(var + eps_norm)).astype(jnp.bfloat16)
    query = head_norm(jnp.dot(normed, qkv_weight[0], preferred_element_type=jnp.float32))
    keys = head_norm(jnp.dot(normed, qkv_weight[1], preferred_element_type=jnp.float32))
    values = jnp.dot(normed, qkv_weight[2], preferred_element_type=jnp.float32).astype(jnp.bfloat16)
    attn = attend_pack(query, keys, values, image)
    mixed = jnp.dot(attn, out_weight, preferred_element_type=jnp.float32).astype(jnp.bfloat16)
    picks = (starts[:, None] + jnp.remainder(latent_index, lengths[:, None])).astype(jnp.int32)
    picked = mixed[picks.reshape(-1)].reshape(IMAGES, LAT, D)
    latents = jnp.zeros((IMAGES, LAT, D), jnp.bfloat16).at[owner_slot].set(picked).reshape(IMAGES * LAT, D)
    grad = lax.dot_general(attn, cotangent, (((0,), (0,)), ((), ())), preferred_element_type=jnp.float32)
    return (mixed, latents, grad)

def reference(tokens, lengths, owner_slot, latent_index, cotangent, qkv_weight, out_weight):
    mixed_all = []
    latent_all = []
    grad_total = jnp.zeros((D, D), jnp.float32)
    for pack in range(PACKS):
        mixed, latents, grad = one_pack(tokens[pack], lengths[pack], owner_slot[pack], latent_index[pack], cotangent[pack], qkv_weight, out_weight)
        mixed_all.append(mixed)
        latent_all.append(latents)
        grad_total = grad_total + grad
    grad_out = grad_total * (PACKS * S) ** (-0.5)
    return (jnp.stack(mixed_all), jnp.stack(latent_all), grad_out)
```

```python
import functools

import jax
import jax.numpy as jnp
from jax import lax
from jax.experimental import pallas as pl
from jax.experimental.pallas import tpu as pltpu
from jax.sharding import Mesh
from jax.sharding import PartitionSpec as P

HD = 64
LAT = 128
GROUP = 256
BIG = 128.0
EPS_NORM = 1e-05
EPS_HEAD = 1e-06
BF = jnp.bfloat16
F32 = jnp.float32
PLANE = ("seq", "y", "xl")
VMEM_LIMIT = 48 * 1024 * 1024


def norm_rows(head, own_ref, oth_ref, normed_ref, rows):
    share = own_ref.shape[1]
    step = 64

    def one(i, carry):
        at = pl.ds(pl.multiple_of(i * step, step), step)
        own = own_ref[at, :].astype(F32)
        oth = oth_ref[at, :].astype(F32)
        inv = 1.0 / (2 * share)
        mean = (jnp.sum(own, axis=1, keepdims=True) + jnp.sum(oth, axis=1, keepdims=True)) * inv
        own = own - mean
        oth = oth - mean
        var = (jnp.sum(own * own, axis=1, keepdims=True) + jnp.sum(oth * oth, axis=1, keepdims=True)) * inv
        scale = lax.rsqrt(var + EPS_NORM)
        own = (own * scale).astype(BF)
        oth = (oth * scale).astype(BF)

        @pl.when(head == 0)
        def _():
            normed_ref[at, :share] = own
            normed_ref[at, share:] = oth

        @pl.when(head != 0)
        def _():
            normed_ref[at, :share] = oth
            normed_ref[at, share:] = own

        return carry

    lax.fori_loop(0, rows // step, one, 0)


def head_norm(values, ones):
    square = values * values
    high = square.astype(BF)
    low = (square - high.astype(F32)).astype(BF)
    mean = jnp.dot(high, ones, preferred_element_type=F32) + jnp.dot(low, ones, preferred_element_type=F32)
    return values * lax.rsqrt(mean + EPS_HEAD)


def ones_block():
    row = lax.broadcasted_iota(jnp.int32, (GROUP, GROUP), 0) // HD
    col = lax.broadcasted_iota(jnp.int32, (GROUP, GROUP), 1) // HD
    return jnp.where(row == col, 1.0 / HD, 0.0).astype(BF)


def features(bounds_ref, first, rows, inside, constant):
    pos = first + lax.broadcasted_iota(jnp.int32, (rows, 128), 0)
    lane = lax.broadcasted_iota(jnp.int32, (rows, 128), 1) & (HD - 1)
    member = (pos >= bounds_ref[0:1, :]) & (pos < bounds_ref[1:2, :])
    return jnp.where(lane == 8, constant, jnp.where(member, inside, 0.0)).astype(BF)


def lower_half(rows):
    return lax.broadcasted_iota(jnp.int32, (rows, 128), 1) < HD


def attend_group(q, k, v, qfeat, kfeat, emit):
    q = (q.astype(F32) * 0.125).astype(BF)
    for pair in range(2):
        lanes = slice(pair * 128, pair * 128 + 128)
        qp, kp, vp = q[:, lanes], k[:, lanes], v[:, lanes]
        qlow, klow = lower_half(qp.shape[0]), lower_half(kp.shape[0])
        one = jnp.ones_like(vp)
        for odd in range(2):
            qa = jnp.where(qlow, qfeat, qp) if odd else jnp.where(qlow, qp, qfeat)
            ka = jnp.where(klow, kfeat, kp) if odd else jnp.where(klow, kp, kfeat)
            va = jnp.where(klow, one, vp) if odd else jnp.where(klow, vp, one)
            s = lax.dot_general(qa, ka, (((1,), (1,)), ((), ())), preferred_element_type=F32)
            w = jnp.exp(s).astype(BF)
            emit(2 * pair + odd, jnp.dot(w, va, preferred_element_type=F32))


def local_kernel(place_ref, bounds_ref, own_ref, oth_ref, w_ref, q_ref, acc_ref, normed_ref, qf_ref, kf_ref, ones_ref):
    rows = own_ref.shape[0]

    @pl.when(pl.program_id(0) == 0)
    def _():
        norm_rows(place_ref[1], own_ref, oth_ref, normed_ref, rows)
        first = place_ref[0] * rows
        qf_ref[...] = features(bounds_ref, first, rows, BIG, -BIG)
        kf_ref[...] = features(bounds_ref, first, rows, 1.0, 1.0)
        ones_ref[...] = ones_block()

    normed = normed_ref[...]
    ones = ones_ref[...]
    q = head_norm(jnp.dot(normed, w_ref[0], preferred_element_type=F32), ones).astype(BF)
    k = head_norm(jnp.dot(normed, w_ref[1], preferred_element_type=F32), ones).astype(BF)
    v = jnp.dot(normed, w_ref[2], preferred_element_type=F32).astype(BF)
    q_ref[...] = q

    def emit(head, r):
        acc_ref[:, head * 128 : head * 128 + 128] = r

    attend_group(q, k, v, qf_ref[...], kf_ref[...], emit)


def near_kernel(place_ref, bounds_ref, own_ref, oth_ref, wk_ref, wv_ref, q_ref, acc_in_ref, acc_ref, normed_ref, qf_ref, kf_ref, ones_ref):
    rows = own_ref.shape[0]
    span = q_ref.shape[0]

    @pl.when(pl.program_id(0) == 0)
    def _():
        norm_rows(place_ref[1], own_ref, oth_ref, normed_ref, rows)
        qf_ref[...] = features(bounds_ref, place_ref[0] * span, span, BIG, -BIG)
        kf_ref[...] = features(bounds_ref, jnp.where(place_ref[0] == 0, span, span - rows), rows, 1.0, 1.0)
        ones_ref[...] = ones_block()

    normed = normed_ref[...]
    k = head_norm(jnp.dot(normed, wk_ref[0], preferred_element_type=F32), ones_ref[...]).astype(BF)
    v = jnp.dot(normed, wv_ref[0], preferred_element_type=F32).astype(BF)

    def emit(head, r):
        lanes = slice(head * 128, head * 128 + 128)
        acc_ref[:, lanes] = acc_in_ref[:, lanes] + r

    attend_group(q_ref[...], k, v, qf_ref[...], kf_ref[...], emit)


def far_kernel(place_ref, bounds_ref, own_ref, oth_ref, wk_ref, wv_ref, q_ref, acc_in_ref, cot_ref, attn_ref, grad_ref, normed_ref, qf_ref, kf_ref, ones_ref, acc_ref):
    rows = own_ref.shape[0]
    span = acc_in_ref.shape[0]
    part = q_ref.shape[0]
    begin = jnp.where(place_ref[0] == 0, span - part, 0)

    @pl.when(pl.program_id(0) == 0)
    def _():
        norm_rows(place_ref[1], own_ref, oth_ref, normed_ref, rows)
        qf_ref[...] = features(bounds_ref, place_ref[0] * span + begin, part, BIG, -BIG)
        kf_ref[...] = features(bounds_ref, jnp.where(place_ref[0] == 0, 2 * span - rows, 0), rows, 1.0, 1.0)
        ones_ref[...] = ones_block()

    normed = normed_ref[...]
    k = head_norm(jnp.dot(normed, wk_ref[0], preferred_element_type=F32), ones_ref[...]).astype(BF)
    v = jnp.dot(normed, wv_ref[0], preferred_element_type=F32).astype(BF)
    acc_ref[...] = acc_in_ref[...]
    at = pl.ds(pl.multiple_of(begin, part), part)

    def emit(head, r):
        lanes = slice(head * 128, head * 128 + 128)
        acc_ref[at, lanes] = acc_ref[at, lanes] + r

    attend_group(q_ref[...], k, v, qf_ref[...], kf_ref[...], emit)
    low = lower_half(span)
    for pair in range(2):
        even = acc_ref[:, pair * 256 : pair * 256 + 128]
        odd = acc_ref[:, pair * 256 + 128 : pair * 256 + 256]
        total = pltpu.roll(jnp.where(low, odd, even), HD, 1)
        attn_ref[:, pair * 128 : pair * 128 + 128] = (jnp.where(low, even, odd) / total).astype(BF)
    grad_ref[...] = lax.dot_general(attn_ref[...], cot_ref[...], (((0,), (0,)), ((), ())), preferred_element_type=F32).astype(BF)


def send_kernel(place_ref, attn_ref, w_ref, out_ref):
    out_ref[...] = jnp.dot(attn_ref[...], w_ref[...], preferred_element_type=F32).astype(BF)


def mixed_kernel(place_ref, attn_ref, w_ref, recv_ref, pick_ref, mixed_ref, send_ref, keep_ref):
    rows = attn_ref.shape[0]
    mixed = (jnp.dot(attn_ref[...], w_ref[...], preferred_element_type=F32) + recv_ref[...].astype(F32)).astype(BF)
    mixed_ref[...] = mixed
    row = lax.broadcasted_iota(jnp.int32, (rows, rows), 1)
    for half, out in ((0, send_ref), (1, keep_ref)):
        hot = jnp.where(pick_ref[half * rows : half * rows + rows, :] == row, 1.0, 0.0).astype(BF)
        out[...] = jnp.dot(hot, mixed, preferred_element_type=F32).astype(BF)


def call(kernel, place, grid, in_specs, out_specs, out_shape, scratch, flops, nbytes, args, alias=None):
    return pl.pallas_call(
        kernel,
        grid_spec=pltpu.PrefetchScalarGridSpec(
            num_scalar_prefetch=1, grid=grid, in_specs=in_specs, out_specs=out_specs, scratch_shapes=scratch
        ),
        out_shape=out_shape,
        input_output_aliases=alias or {},
        cost_estimate=pl.CostEstimate(flops=flops, bytes_accessed=nbytes, transcendentals=0),
        compiler_params=pltpu.CompilerParams(vmem_limit_bytes=VMEM_LIMIT),
    )(place, *args)


def whole(shape):
    return pl.BlockSpec(shape, lambda g, s: (0,) * len(shape))


def columns(rows, width):
    return pl.BlockSpec((rows, width), lambda g, s: (0, g))


def swap(value, axis):
    return lax.ppermute(value, axis, [(0, 1), (1, 0)])


def sum_parts(parts):
    return jnp.sum(parts.astype(F32), axis=0).astype(BF)


def reduce_grad(grad):
    rows, width = grad.shape
    n = 1
    for axis in PLANE:
        n *= lax.axis_size(axis)
    nz = lax.axis_size("z")
    chunks = 3
    span = rows // chunks
    pieces = []
    for c in range(chunks):
        part = grad[c * span : c * span + span].reshape(n, span // n, width)
        got = lax.all_to_all(part, PLANE, 0, 0)
        pieces.append(sum_parts(got))
    mine = jnp.concatenate(pieces, axis=0)
    if nz > 1:
        shape = mine.shape
        part = mine.reshape(nz, 8, -1)
        got = sum_parts(lax.all_to_all(part, "z", 0, 0))
        mine = lax.all_gather(got, "z", axis=0).reshape(shape)
    outs = []
    for c in range(chunks):
        small = mine[c * (span // n) : (c + 1) * (span // n)]
        outs.append(lax.all_gather(small, PLANE, axis=0, tiled=True))
    return outs


def body(tokens, lengths, owner_slot, latent_index, cotangent, qkv_weight, out_weight):
    own = tokens[0]
    rows, share = own.shape
    half = rows // 2
    groups = share // GROUP
    seq = lax.axis_index("seq")
    head = lax.axis_index("head")
    place = jnp.stack([seq, head]).astype(jnp.int32)

    near = lax.dynamic_slice_in_dim(own, (1 - seq) * half, half, 0)
    far = lax.dynamic_slice_in_dim(own, seq * half, half, 0)
    near_own = swap(near, "seq")
    far_own = swap(far, "seq")
    oth = swap(own, "head")
    near_oth = swap(near_own, "head")
    far_oth = swap(far_own, "head")

    sizes = lengths[0]
    images = sizes.shape[0]
    ends = jnp.cumsum(sizes, dtype=jnp.int32)
    starts = ends - sizes
    pad = lambda a: jnp.tile(jnp.pad(a, (0, HD - images)), 2)
    bounds = jnp.pad(jnp.stack([pad(starts), pad(ends)]), ((0, 6), (0, 0)))

    scratch = lambda r, qr, kr: [
        pltpu.VMEM((r, 2 * share), BF),
        pltpu.VMEM((qr, 128), BF),
        pltpu.VMEM((kr, 128), BF),
        pltpu.VMEM((GROUP, GROUP), BF),
    ]
    weight = lambda j: pl.BlockSpec((1, 2 * share, GROUP), lambda g, s: (j, 0, g))
    q, acc = call(
        local_kernel, place, (groups,),
        [whole((8, 128)), whole((rows, share)), whole((rows, share)),
         pl.BlockSpec((3, 2 * share, GROUP), lambda g, s: (0, 0, g))],
        [columns(rows, GROUP), columns(rows, 2 * GROUP)],
        [jax.ShapeDtypeStruct((rows, share), BF), jax.ShapeDtypeStruct((rows, 2 * share), F32)],
        scratch(rows, rows, rows), 7 * 10**9, 12 * 10**6, (bounds, own, oth, qkv_weight),
    )
    acc = call(
        near_kernel, place, (groups,),
        [whole((8, 128)), whole((half, share)), whole((half, share)), weight(1), weight(2),
         columns(rows, GROUP), columns(rows, 2 * GROUP)],
        columns(rows, 2 * GROUP),
        jax.ShapeDtypeStruct((rows, 2 * share), F32),
        scratch(half, rows, half), 3 * 10**9, 12 * 10**6,
        (bounds, near_own, near_oth, qkv_weight, qkv_weight, q, acc), {7: 0},
    )
    attn, grad = call(
        far_kernel, place, (groups,),
        [whole((8, 128)), whole((half, share)), whole((half, share)), weight(1), weight(2),
         pl.BlockSpec((half, GROUP), lambda g, s: (1 - s[0], g)), columns(rows, 2 * GROUP), whole((rows, 2 * share))],
        [columns(rows, GROUP), pl.BlockSpec((GROUP, 2 * share), lambda g, s: (g, 0))],
        [jax.ShapeDtypeStruct((rows, share), BF), jax.ShapeDtypeStruct((share, 2 * share), BF)],
        scratch(half, half, half) + [pltpu.VMEM((rows, 2 * GROUP), F32)], 4 * 10**9, 14 * 10**6,
        (bounds, far_own, far_oth, qkv_weight, qkv_weight, q, acc, cotangent[0]),
    )
    sums = reduce_grad(grad)

    partial = call(
        send_kernel, place, (groups,),
        [whole((rows, share)), pl.BlockSpec((share, GROUP), lambda g, s: (0, (1 - s[1]) * groups + g))],
        columns(rows, GROUP), jax.ShapeDtypeStruct((rows, share), BF), [], 6 * 10**8, 3 * 10**6, (attn, out_weight),
    )
    recv = swap(partial, "head")

    slots = owner_slot[0]
    picks = starts[:, None] + jnp.remainder(latent_index[0], sizes[:, None])
    order = slots[None, :] == jnp.arange(images, dtype=jnp.int32)[:, None]
    by_slot = jnp.sum(jnp.where(order[:, :, None], picks[None], 0), axis=1).reshape(2, rows)
    local = by_slot - seq * rows
    local = jnp.stack([jnp.where(seq == 0, local[1], local[0]), jnp.where(seq == 0, local[0], local[1])])
    local = local.reshape(2 * rows, 1)

    shape = jax.ShapeDtypeStruct((rows, share), BF)
    mixed, send, keep = call(
        mixed_kernel, place, (groups,),
        [whole((rows, share)), pl.BlockSpec((share, GROUP), lambda g, s: (0, s[1] * groups + g)),
         columns(rows, GROUP), whole((2 * rows, 1))],
        [columns(rows, GROUP)] * 3, [shape] * 3, [], 14 * 10**8, 6 * 10**6, (attn, out_weight, recv, local),
    )
    latents = keep + swap(send, "seq")

    count = 2 * rows * lax.axis_size("z") * lax.axis_size("y") * lax.axis_size("xl")
    grad_out = jnp.concatenate([s.astype(F32) * count ** (-0.5) for s in sums], axis=0)
    return mixed[None], latents[None], grad_out


def on_mesh(fine):
    dp = ("z", "y", "xl")
    in_specs = (
        P(dp, "seq", "head"),
        P(dp, None),
        P(dp, None),
        P(dp, None, None),
        P(dp, "seq", None),
        P(None, None, "head"),
        P("head", None),
    )
    out_specs = (P(dp, "seq", "head"), P(dp, "seq", "head"), P("head", None))
    return jax.shard_map(body, mesh=fine, in_specs=in_specs, out_specs=out_specs, check_vma=False)


def solution(mesh):
    return on_mesh(Mesh(mesh.devices.reshape(2, 2, 8, 4, 2), ("seq", "head", "z", "y", "xl")))
```

```python
import functools

import jax
import jax.numpy as jnp
from jax import lax
from jax.experimental import pallas as pl
from jax.experimental.pallas import tpu as pltpu
from jax.sharding import Mesh
from jax.sharding import PartitionSpec as P

HD = 64
LAT = 128
GROUP = 256
BIG = 128.0
EPS_NORM = 1e-05
EPS_HEAD = 1e-06
BF = jnp.bfloat16
F32 = jnp.float32
VMEM_LIMIT = 48 * 1024 * 1024


def norm_rows(head, own_ref, oth_ref, normed_ref, rows):
    share = own_ref.shape[1]
    step = 64

    def one(i, carry):
        at = pl.ds(pl.multiple_of(i * step, step), step)
        own = own_ref[at, :].astype(F32)
        oth = oth_ref[at, :].astype(F32)
        inv = 1.0 / (2 * share)
        mean = (jnp.sum(own, axis=1, keepdims=True) + jnp.sum(oth, axis=1, keepdims=True)) * inv
        own = own - mean
        oth = oth - mean
        var = (jnp.sum(own * own, axis=1, keepdims=True) + jnp.sum(oth * oth, axis=1, keepdims=True)) * inv
        scale = lax.rsqrt(var + EPS_NORM)
        own = (own * scale).astype(BF)
        oth = (oth * scale).astype(BF)

        @pl.when(head == 0)
        def _():
            normed_ref[at, :share] = own
            normed_ref[at, share:] = oth

        @pl.when(head != 0)
        def _():
            normed_ref[at, :share] = oth
            normed_ref[at, share:] = own

        return carry

    lax.fori_loop(0, rows // step, one, 0)


def head_norm(values, ones):
    mean = jnp.dot((values * values).astype(BF), ones, preferred_element_type=F32)
    return values * lax.rsqrt(mean + EPS_HEAD)


def ones_block():
    row = lax.broadcasted_iota(jnp.int32, (GROUP, GROUP), 0) // HD
    col = lax.broadcasted_iota(jnp.int32, (GROUP, GROUP), 1) // HD
    return jnp.where(row == col, 1.0 / HD, 0.0).astype(BF)


def features(bounds_ref, first, rows, inside, constant):
    pos = first + lax.broadcasted_iota(jnp.int32, (rows, 128), 0)
    lane = lax.broadcasted_iota(jnp.int32, (rows, 128), 1) & (HD - 1)
    member = (pos >= bounds_ref[0:1, :]) & (pos < bounds_ref[1:2, :])
    return jnp.where(lane == 8, constant, jnp.where(member, inside, 0.0)).astype(BF)


def lower_half(rows):
    return lax.broadcasted_iota(jnp.int32, (rows, 128), 1) < HD


def attend_group(q, k, v, qfeat, kfeat, emit):
    q = (q.astype(F32) * 0.125).astype(BF)
    for pair in range(2):
        lanes = slice(pair * 128, pair * 128 + 128)
        qp, kp, vp = q[:, lanes], k[:, lanes], v[:, lanes]
        qlow, klow = lower_half(qp.shape[0]), lower_half(kp.shape[0])
        one = jnp.ones_like(vp)
        for odd in range(2):
            qa = jnp.where(qlow, qfeat, qp) if odd else jnp.where(qlow, qp, qfeat)
            ka = jnp.where(klow, kfeat, kp) if odd else jnp.where(klow, kp, kfeat)
            va = jnp.where(klow, one, vp) if odd else jnp.where(klow, vp, one)
            s = lax.dot_general(qa, ka, (((1,), (1,)), ((), ())), preferred_element_type=F32)
            w = jnp.exp(s).astype(BF)
            emit(2 * pair + odd, jnp.dot(w, va, preferred_element_type=F32))


def local_kernel(place_ref, bounds_ref, own_ref, oth_ref, w_ref, q_ref, acc_ref, normed_ref, qf_ref, kf_ref, ones_ref):
    rows = own_ref.shape[0]

    @pl.when(pl.program_id(0) == 0)
    def _():
        norm_rows(place_ref[1], own_ref, oth_ref, normed_ref, rows)
        first = place_ref[0] * rows
        qf_ref[...] = features(bounds_ref, first, rows, BIG, -BIG)
        kf_ref[...] = features(bounds_ref, first, rows, 1.0, 1.0)
        ones_ref[...] = ones_block()

    normed = normed_ref[...]
    ones = ones_ref[...]
    q = head_norm(jnp.dot(normed, w_ref[0], preferred_element_type=F32), ones).astype(BF)
    k = head_norm(jnp.dot(normed, w_ref[1], preferred_element_type=F32), ones).astype(BF)
    v = jnp.dot(normed, w_ref[2], preferred_element_type=F32).astype(BF)
    q_ref[...] = q

    def emit(head, r):
        acc_ref[:, head * 128 : head * 128 + 128] = r

    attend_group(q, k, v, qf_ref[...], kf_ref[...], emit)


def foreign_kernel(place_ref, bounds_ref, own_ref, oth_ref, wk_ref, wv_ref, q_ref, acc_in_ref, attn_ref, turned_ref, normed_ref, qf_ref, kf_ref, ones_ref, k_ref, v_ref, acc_ref):
    rows = own_ref.shape[0]
    half = rows // 2

    @pl.when(pl.program_id(0) == 0)
    def _():
        norm_rows(place_ref[1], own_ref, oth_ref, normed_ref, rows)
        qf_ref[...] = features(bounds_ref, place_ref[0] * rows, rows, BIG, -BIG)
        kf_ref[...] = features(bounds_ref, (1 - place_ref[0]) * rows, rows, 1.0, 1.0)
        ones_ref[...] = ones_block()

    normed = normed_ref[...]
    k_ref[...] = head_norm(jnp.dot(normed, wk_ref[0], preferred_element_type=F32), ones_ref[...]).astype(BF)
    v_ref[...] = jnp.dot(normed, wv_ref[0], preferred_element_type=F32).astype(BF)
    near = pl.ds(pl.multiple_of(place_ref[0] * half, half), half)
    far = pl.ds(pl.multiple_of((1 - place_ref[0]) * half, half), half)

    def emit_near(head, r):
        lanes = slice(head * 128, head * 128 + 128)
        acc_ref[:, lanes] = acc_in_ref[:, lanes] + r

    attend_group(q_ref[...], k_ref[near, :], v_ref[near, :], qf_ref[...], kf_ref[near, :], emit_near)

    def emit_far(head, r):
        lanes = slice(head * 128, head * 128 + 128)
        acc_ref[far, lanes] = acc_ref[far, lanes] + r

    attend_group(q_ref[far, :], k_ref[far, :], v_ref[far, :], qf_ref[far, :], kf_ref[far, :], emit_far)
    low = lower_half(rows)
    for pair in range(2):
        even = acc_ref[:, pair * 256 : pair * 256 + 128]
        odd = acc_ref[:, pair * 256 + 128 : pair * 256 + 256]
        total = pltpu.roll(jnp.where(low, odd, even), HD, 1)
        attn_ref[:, pair * 128 : pair * 128 + 128] = (jnp.where(low, even, odd) / total).astype(BF)
    turned_ref[...] = attn_ref[...].T


def send_kernel(place_ref, attn_ref, w_ref, out_ref):
    out_ref[...] = jnp.dot(attn_ref[...], w_ref[...], preferred_element_type=F32).astype(BF)


def mixed_kernel(place_ref, attn_ref, w_ref, recv_ref, pick_ref, mixed_ref, send_ref, keep_ref):
    rows = attn_ref.shape[0]
    mixed = (jnp.dot(attn_ref[...], w_ref[...], preferred_element_type=F32) + recv_ref[...].astype(F32)).astype(BF)
    mixed_ref[...] = mixed
    row = lax.broadcasted_iota(jnp.int32, (rows, rows), 1)
    for half, out in ((0, send_ref), (1, keep_ref)):
        hot = jnp.where(pick_ref[half * rows : half * rows + rows, :] == row, 1.0, 0.0).astype(BF)
        out[...] = jnp.dot(hot, mixed, preferred_element_type=F32).astype(BF)


def call(kernel, place, grid, in_specs, out_specs, out_shape, scratch, flops, nbytes, args, alias=None):
    return pl.pallas_call(
        kernel,
        grid_spec=pltpu.PrefetchScalarGridSpec(
            num_scalar_prefetch=1, grid=grid, in_specs=in_specs, out_specs=out_specs, scratch_shapes=scratch
        ),
        out_shape=out_shape,
        input_output_aliases=alias or {},
        cost_estimate=pl.CostEstimate(flops=flops, bytes_accessed=nbytes, transcendentals=0),
        compiler_params=pltpu.CompilerParams(vmem_limit_bytes=VMEM_LIMIT),
    )(place, *args)


def whole(shape):
    return pl.BlockSpec(shape, lambda g, s: (0,) * len(shape))


def columns(rows, width):
    return pl.BlockSpec((rows, width), lambda g, s: (0, g))


def swap(value, axis):
    return lax.ppermute(value, axis, [(0, 1), (1, 0)])


def grad_kernel(mask_ref, turned_ref, cot_ref, send_ref, keep_ref):
    mask = mask_ref[0]
    eight, piece, _ = send_ref.shape
    top = mask >> 3
    block = 4 * piece
    for out, upper in ((send_ref, 1 - top), (keep_ref, top)):
        for b in range(2):
            first = pl.multiple_of(upper * eight * piece + b * block, piece)
            got = jnp.dot(turned_ref[pl.ds(first, block), :], cot_ref[...], preferred_element_type=F32).astype(BF)
            for i in range(4):
                out[(b * 4 + i) ^ (mask & 7)] = got[i * piece : i * piece + piece]


def place_kernel(mask_ref, lower0_ref, upper0_ref, lower1_ref, upper1_ref, out_ref, *, scale):
    _, piece, width = lower0_ref.shape
    for i in range(2):
        rows = slice(i * piece, i * piece + piece)
        for c, (lower, upper) in enumerate(((lower0_ref, upper0_ref), (lower1_ref, upper1_ref))):
            at = (pl.program_id(0) * 2 + i) ^ mask_ref[c]
            cols = slice(c * width, c * width + width)

            @pl.when(at < 8)
            def _():
                out_ref[rows, cols] = lower[at & 7].astype(F32) * scale

            @pl.when(at >= 8)
            def _():
                out_ref[rows, cols] = upper[at & 7].astype(F32) * scale


AXES = ("seq", "head", "z", "y", "xl")
ROUTES = (
    ((("y", 0), ("y", 1), ("z", 0), ("z", 1)), (("z", 0), ("z", 1), ("y", 0), ("y", 1))),
    ((("z", 1), ("z", 0), ("y", 1), ("y", 0)), (("y", 1), ("y", 0), ("z", 1), ("z", 0))),
)


def across(i, kind, n):
    if kind == 0:
        return i ^ 1
    return (i + 1) % n if i % 2 else (i - 1) % n


def bit_of(i, kind):
    return ((i + 1) >> 1) & 1 if kind == 0 else (i >> 1) & 1


def every_device(sizes):
    for i in range(sizes[0] * sizes[1] * sizes[2] * sizes[3] * sizes[4]):
        at, rest = {}, i
        for name, n in reversed(list(zip(AXES, sizes))):
            at[name] = rest % n
            rest //= n
        yield i, at


def index_of(at, sizes):
    i = 0
    for name, n in zip(AXES, sizes):
        i = i * n + at[name]
    return i


def pairs(sizes, partner):
    out = []
    for i, at in every_device(sizes):
        out.append((i, index_of(partner(at), sizes)))
    return out


def pair_table(sizes, chunk, stage):
    n = dict(zip(AXES, sizes))

    def partner(at):
        axis, kind = ROUTES[chunk][at["head"]][stage]
        return {**at, axis: across(at[axis], kind, n[axis])}

    return pairs(sizes, partner)


def last_tables(sizes):
    n = dict(zip(AXES, sizes))
    x = lambda at: at["seq"] * n["xl"] + at["xl"]
    tables = []
    for kind in (0, 1):
        def partner(at, kind=kind):
            to = across(x(at), kind, n["seq"] * n["xl"])
            return {**at, "seq": to // n["xl"], "xl": to % n["xl"]}

        tables.append(pairs(sizes, partner))
    tables.append(pairs(sizes, lambda at: {**at, "z": (at["z"] + n["z"] // 2) % n["z"]}))
    return tables


def mask_of(chunk, head):
    masks = []
    for core in (0, 1):
        mask = jnp.int32(0)
        for axis, kind in ROUTES[chunk][core]:
            mask = mask * 2 + bit_of(lax.axis_index(axis).astype(jnp.int32), kind)
        masks.append(mask)
    return jnp.where(head == 0, masks[0], masks[1])


def add(a, b):
    return (a.astype(F32) + b.astype(F32)).astype(BF)


def reduce_grad(turned, cot, scale, head):
    share, width = turned.shape[0], cot.shape[1]
    sizes = tuple(lax.axis_size(a) for a in AXES)
    masks = [mask_of(c, head) for c in range(2)]
    piece = share // 16
    half = jax.ShapeDtypeStruct((8, piece, width // 2), BF)
    move = lambda value, table: lax.ppermute(value, AXES, table)
    held = []
    for c in range(2):
        held.append(list(call(
            grad_kernel, masks[c][None], (1,),
            [whole(turned.shape), pl.BlockSpec((cot.shape[0], width // 2), lambda g, s, c=c: (0, c))],
            [whole(half.shape)] * 2, [half] * 2, [], 6 * 10**8, 4 * 10**6, (turned, cot),
        )))
    for stage in range(4):
        for c in range(2):
            send, keep = held[c]
            got = move(send, pair_table(sizes, c, stage))
            n = keep.shape[0] // 2
            if n:
                held[c] = [add(keep[n:], got[n:]), add(keep[:n], got[:n])]
            else:
                held[c] = add(keep, got)
    both = jnp.concatenate(held, axis=0)
    for table in last_tables(sizes):
        both = add(both, move(both, table))
    lower = [both[0:1], both[1:2]]
    upper = [None, None]
    for stage in (3, 2, 1, 0):
        for c in range(2):
            if upper[c] is not None:
                lower[c] = jnp.concatenate([lower[c], upper[c]], axis=0)
            upper[c] = move(lower[c], pair_table(sizes, c, stage))
    return call(
        functools.partial(place_kernel, scale=scale), jnp.stack(masks), (8,),
        [whole(half.shape)] * 4, pl.BlockSpec((2 * piece, width), lambda g, s: (g, 0)),
        jax.ShapeDtypeStruct((share, width), F32), [], 10**6, 7 * 10**6,
        (lower[0], upper[0], lower[1], upper[1]),
    )


def body(tokens, lengths, owner_slot, latent_index, cotangent, qkv_weight, out_weight):
    own = tokens[0]
    rows, share = own.shape
    groups = share // GROUP
    seq = lax.axis_index("seq")
    head = lax.axis_index("head")
    place = jnp.stack([seq, head]).astype(jnp.int32)

    oth = swap(own, "head")
    foreign_own = swap(own, "seq")

    sizes = lengths[0]
    images = sizes.shape[0]
    ends = jnp.cumsum(sizes, dtype=jnp.int32)
    starts = ends - sizes
    pad = lambda a: jnp.tile(jnp.pad(a, (0, HD - images)), 2)
    bounds = jnp.pad(jnp.stack([pad(starts), pad(ends)]), ((0, 6), (0, 0)))

    scratch = lambda r, qr, kr: [
        pltpu.VMEM((r, 2 * share), BF),
        pltpu.VMEM((qr, 128), BF),
        pltpu.VMEM((kr, 128), BF),
        pltpu.VMEM((GROUP, GROUP), BF),
    ]
    weight = lambda j: pl.BlockSpec((1, 2 * share, GROUP), lambda g, s: (j, 0, g))
    q, acc = call(
        local_kernel, place, (groups,),
        [whole((8, 128)), whole((rows, share)), whole((rows, share)),
         pl.BlockSpec((3, 2 * share, GROUP), lambda g, s: (0, 0, g))],
        [columns(rows, GROUP), columns(rows, 2 * GROUP)],
        [jax.ShapeDtypeStruct((rows, share), BF), jax.ShapeDtypeStruct((rows, 2 * share), F32)],
        scratch(rows, rows, rows), 7 * 10**9, 12 * 10**6, (bounds, own, oth, qkv_weight),
    )
    foreign_own, q = lax.optimization_barrier((foreign_own, q))
    foreign_oth = swap(foreign_own, "head")
    attn, turned = call(
        foreign_kernel, place, (groups,),
        [whole((8, 128)), whole((rows, share)), whole((rows, share)), weight(1), weight(2),
         columns(rows, GROUP), columns(rows, 2 * GROUP)],
        [columns(rows, GROUP), pl.BlockSpec((GROUP, rows), lambda g, s: (g, 0))],
        [jax.ShapeDtypeStruct((rows, share), BF), jax.ShapeDtypeStruct((share, rows), BF)],
        scratch(rows, rows, rows)
        + [pltpu.VMEM((rows, GROUP), BF), pltpu.VMEM((rows, GROUP), BF), pltpu.VMEM((rows, 2 * GROUP), F32)],
        4 * 10**9, 14 * 10**6, (bounds, foreign_own, foreign_oth, qkv_weight, qkv_weight, q, acc),
    )
    count = 2 * rows * lax.axis_size("z") * lax.axis_size("y") * lax.axis_size("xl")
    grad_out = reduce_grad(turned, cotangent[0], count ** (-0.5), head)

    partial = call(
        send_kernel, place, (groups,),
        [whole((rows, share)), pl.BlockSpec((share, GROUP), lambda g, s: (0, (1 - s[1]) * groups + g))],
        columns(rows, GROUP), jax.ShapeDtypeStruct((rows, share), BF), [], 6 * 10**8, 3 * 10**6, (attn, out_weight),
    )
    recv = swap(partial, "head")

    slots = owner_slot[0]
    picks = starts[:, None] + jnp.remainder(latent_index[0], sizes[:, None])
    order = slots[None, :] == jnp.arange(images, dtype=jnp.int32)[:, None]
    by_slot = jnp.sum(jnp.where(order[:, :, None], picks[None], 0), axis=1).reshape(2, rows)
    local = by_slot - seq * rows
    local = jnp.stack([jnp.where(seq == 0, local[1], local[0]), jnp.where(seq == 0, local[0], local[1])])
    local = local.reshape(2 * rows, 1)

    shape = jax.ShapeDtypeStruct((rows, share), BF)
    mixed, send, keep = call(
        mixed_kernel, place, (groups,),
        [whole((rows, share)), pl.BlockSpec((share, GROUP), lambda g, s: (0, s[1] * groups + g)),
         columns(rows, GROUP), whole((2 * rows, 1))],
        [columns(rows, GROUP)] * 3, [shape] * 3, [], 14 * 10**8, 6 * 10**6, (attn, out_weight, recv, local),
    )
    latents = keep + swap(send, "seq")

    return mixed[None], latents[None], grad_out


def on_mesh(fine):
    dp = ("z", "y", "xl")
    in_specs = (
        P(dp, "seq", "head"),
        P(dp, None),
        P(dp, None),
        P(dp, None, None),
        P(dp, "seq", None),
        P(None, None, "head"),
        P("head", None),
    )
    out_specs = (P(dp, "seq", "head"), P(dp, "seq", "head"), P("head", None))
    return jax.shard_map(body, mesh=fine, in_specs=in_specs, out_specs=out_specs, check_vma=False)


def solution(mesh):
    return on_mesh(Mesh(mesh.devices.reshape(2, 2, 8, 4, 2), ("seq", "head", "z", "y", "xl")))
```

```python
import functools

import jax
import jax.numpy as jnp
from jax import lax
from jax.experimental import pallas as pl
from jax.experimental.pallas import tpu as pltpu
from jax.sharding import Mesh
from jax.sharding import PartitionSpec as P

HD = 64
LAT = 128
GROUP = 256
BIG = 128.0
EPS_NORM = 1e-05
EPS_HEAD = 1e-06
BF = jnp.bfloat16
F32 = jnp.float32
VMEM_LIMIT = 20 * 1024 * 1024
FULL_VMEM = 60 * 1024 * 1024


def norm_rows(head, own_ref, oth_ref, normed_ref, rows):
    share = own_ref.shape[1]
    step = 64

    def one(i, carry):
        at = pl.ds(pl.multiple_of(i * step, step), step)
        own = own_ref[at, :].astype(F32)
        oth = oth_ref[at, :].astype(F32)
        inv = 1.0 / (2 * share)
        mean = (jnp.sum(own, axis=1, keepdims=True) + jnp.sum(oth, axis=1, keepdims=True)) * inv
        own = own - mean
        oth = oth - mean
        var = (jnp.sum(own * own, axis=1, keepdims=True) + jnp.sum(oth * oth, axis=1, keepdims=True)) * inv
        scale = lax.rsqrt(var + EPS_NORM)
        own = (own * scale).astype(BF)
        oth = (oth * scale).astype(BF)

        @pl.when(head == 0)
        def _():
            normed_ref[at, :share] = own
            normed_ref[at, share:] = oth

        @pl.when(head != 0)
        def _():
            normed_ref[at, :share] = oth
            normed_ref[at, share:] = own

        return carry

    lax.fori_loop(0, rows // step, one, 0)


def head_norm(values, ones):
    mean = jnp.dot((values * values).astype(BF), ones, preferred_element_type=F32)
    return values * lax.rsqrt(mean + EPS_HEAD)


def ones_block():
    row = lax.broadcasted_iota(jnp.int32, (GROUP, GROUP), 0) // HD
    col = lax.broadcasted_iota(jnp.int32, (GROUP, GROUP), 1) // HD
    return jnp.where(row == col, 1.0 / HD, 0.0).astype(BF)


def features(bounds_ref, first, rows, inside, constant):
    pos = first + lax.broadcasted_iota(jnp.int32, (rows, 128), 0)
    lane = lax.broadcasted_iota(jnp.int32, (rows, 128), 1) & (HD - 1)
    member = (pos >= bounds_ref[0:1, :]) & (pos < bounds_ref[1:2, :])
    return jnp.where(lane == 8, constant, jnp.where(member, inside, 0.0)).astype(BF)


def lower_half(rows):
    return lax.broadcasted_iota(jnp.int32, (rows, 128), 1) < HD


def attend_group(q, k, v, qfeat, kfeat, emit):
    q = (q.astype(F32) * 0.125).astype(BF)
    for pair in range(2):
        lanes = slice(pair * 128, pair * 128 + 128)
        qp, kp, vp = q[:, lanes], k[:, lanes], v[:, lanes]
        qlow, klow = lower_half(qp.shape[0]), lower_half(kp.shape[0])
        one = jnp.ones_like(vp)
        for odd in range(2):
            qa = jnp.where(qlow, qfeat, qp) if odd else jnp.where(qlow, qp, qfeat)
            ka = jnp.where(klow, kfeat, kp) if odd else jnp.where(klow, kp, kfeat)
            va = jnp.where(klow, one, vp) if odd else jnp.where(klow, vp, one)
            s = lax.dot_general(qa, ka, (((1,), (1,)), ((), ())), preferred_element_type=F32)
            w = jnp.exp(s).astype(BF)
            emit(2 * pair + odd, jnp.dot(w, va, preferred_element_type=F32))


def local_kernel(place_ref, bounds_ref, own_ref, oth_ref, w_ref, q_ref, acc_ref, normed_ref, qf_ref, kf_ref, ones_ref):
    rows = own_ref.shape[0]

    @pl.when(pl.program_id(0) == 0)
    def _():
        norm_rows(place_ref[1], own_ref, oth_ref, normed_ref, rows)
        first = place_ref[0] * rows
        qf_ref[...] = features(bounds_ref, first, rows, BIG, -BIG)
        kf_ref[...] = features(bounds_ref, first, rows, 1.0, 1.0)
        ones_ref[...] = ones_block()

    normed = normed_ref[...]
    ones = ones_ref[...]
    q = head_norm(jnp.dot(normed, w_ref[0], preferred_element_type=F32), ones).astype(BF)
    k = head_norm(jnp.dot(normed, w_ref[1], preferred_element_type=F32), ones).astype(BF)
    v = jnp.dot(normed, w_ref[2], preferred_element_type=F32).astype(BF)
    q_ref[...] = q

    def emit(head, r):
        acc_ref[:, head * 128 : head * 128 + 128] = r

    attend_group(q, k, v, qf_ref[...], kf_ref[...], emit)


def foreign_kernel(place_ref, bounds_ref, own_ref, oth_ref, wk_ref, wv_ref, q_ref, acc_in_ref, attn_ref, turned_ref, normed_ref, qf_ref, kf_ref, ones_ref, k_ref, v_ref, acc_ref):
    rows = own_ref.shape[0]
    half = rows // 2

    @pl.when(pl.program_id(0) == 0)
    def _():
        norm_rows(place_ref[1], own_ref, oth_ref, normed_ref, rows)
        qf_ref[...] = features(bounds_ref, place_ref[0] * rows, rows, BIG, -BIG)
        kf_ref[...] = features(bounds_ref, (1 - place_ref[0]) * rows, rows, 1.0, 1.0)
        ones_ref[...] = ones_block()

    normed = normed_ref[...]
    k_ref[...] = head_norm(jnp.dot(normed, wk_ref[0], preferred_element_type=F32), ones_ref[...]).astype(BF)
    v_ref[...] = jnp.dot(normed, wv_ref[0], preferred_element_type=F32).astype(BF)
    near = pl.ds(pl.multiple_of(place_ref[0] * half, half), half)
    far = pl.ds(pl.multiple_of((1 - place_ref[0]) * half, half), half)

    def emit_near(head, r):
        lanes = slice(head * 128, head * 128 + 128)
        acc_ref[:, lanes] = acc_in_ref[:, lanes] + r

    attend_group(q_ref[...], k_ref[near, :], v_ref[near, :], qf_ref[...], kf_ref[near, :], emit_near)

    def emit_far(head, r):
        lanes = slice(head * 128, head * 128 + 128)
        acc_ref[far, lanes] = acc_ref[far, lanes] + r

    attend_group(q_ref[far, :], k_ref[far, :], v_ref[far, :], qf_ref[far, :], kf_ref[far, :], emit_far)
    low = lower_half(rows)
    for pair in range(2):
        even = acc_ref[:, pair * 256 : pair * 256 + 128]
        odd = acc_ref[:, pair * 256 + 128 : pair * 256 + 256]
        total = pltpu.roll(jnp.where(low, odd, even), HD, 1)
        attn_ref[:, pair * 128 : pair * 128 + 128] = (jnp.where(low, even, odd) / total).astype(BF)
    turned_ref[...] = attn_ref[...].T


def send_kernel(place_ref, attn_ref, w_ref, out_ref):
    out_ref[...] = jnp.dot(attn_ref[...], w_ref[...], preferred_element_type=F32).astype(BF)


def mixed_kernel(place_ref, attn_ref, w_ref, recv_ref, pick_ref, mixed_ref, send_ref, keep_ref):
    rows = attn_ref.shape[0]
    mixed = (jnp.dot(attn_ref[...], w_ref[...], preferred_element_type=F32) + recv_ref[...].astype(F32)).astype(BF)
    mixed_ref[...] = mixed
    row = lax.broadcasted_iota(jnp.int32, (rows, rows), 1)
    for half, out in ((0, send_ref), (1, keep_ref)):
        hot = jnp.where(pick_ref[half * rows : half * rows + rows, :] == row, 1.0, 0.0).astype(BF)
        out[...] = jnp.dot(hot, mixed, preferred_element_type=F32).astype(BF)


def call(kernel, place, grid, in_specs, out_specs, out_shape, scratch, flops, nbytes, args, alias=None, limit=VMEM_LIMIT):
    return pl.pallas_call(
        kernel,
        grid_spec=pltpu.PrefetchScalarGridSpec(
            num_scalar_prefetch=1, grid=grid, in_specs=in_specs, out_specs=out_specs, scratch_shapes=scratch
        ),
        out_shape=out_shape,
        input_output_aliases=alias or {},
        cost_estimate=pl.CostEstimate(flops=flops, bytes_accessed=nbytes, transcendentals=0),
        compiler_params=pltpu.CompilerParams(vmem_limit_bytes=limit),
    )(place, *args)


def whole(shape):
    return pl.BlockSpec(shape, lambda g, s: (0,) * len(shape))


def columns(rows, width):
    return pl.BlockSpec((rows, width), lambda g, s: (0, g))


def swap(value, axis):
    return lax.ppermute(value, axis, [(0, 1), (1, 0)])


def grad_kernel(mask_ref, turned_ref, cot_ref, *out_refs):
    mask = mask_ref[0]
    _, piece, _ = out_refs[0].shape
    for out, places in zip(out_refs, (3, 2, 1, 0)):
        first = pl.multiple_of(((mask >> 2) ^ places) * (4 * piece), 4 * piece)
        got = jnp.dot(turned_ref[pl.ds(first, 4 * piece), :], cot_ref[...], preferred_element_type=F32).astype(BF)
        for i in range(4):
            out[i ^ (mask & 3)] = got[i * piece : i * piece + piece]


def place_kernel(mask_ref, *refs, scale, upper):
    out_ref = refs[-1]
    _, piece, _ = refs[0].shape
    for c in range(2):
        mask = mask_ref[c]
        for places in range(2):

            @pl.when((pl.program_id(0) == c) & ((pl.program_id(1) ^ ((mask >> 2) & 1)) == places))
            def _():
                for i in range(4):
                    out_ref[i * piece : i * piece + piece, :] = refs[2 * c + places][i ^ (mask & 3)].astype(F32) * scale


AXES = ("seq", "head", "z", "y", "xl")
ROUTES = (
    ((("y", 0), ("y", 1), ("z", 0), ("z", 1)), (("z", 0), ("z", 1), ("y", 0), ("y", 1))),
    ((("z", 1), ("z", 0), ("y", 1), ("y", 0)), (("y", 1), ("y", 0), ("z", 1), ("z", 0))),
)


def across(i, kind, n):
    if kind == 0:
        return i ^ 1
    return (i + 1) % n if i % 2 else (i - 1) % n


def bit_of(i, kind):
    return ((i + 1) >> 1) & 1 if kind == 0 else (i >> 1) & 1


def every_device(sizes):
    for i in range(sizes[0] * sizes[1] * sizes[2] * sizes[3] * sizes[4]):
        at, rest = {}, i
        for name, n in reversed(list(zip(AXES, sizes))):
            at[name] = rest % n
            rest //= n
        yield i, at


def index_of(at, sizes):
    i = 0
    for name, n in zip(AXES, sizes):
        i = i * n + at[name]
    return i


def pairs(sizes, partner):
    out = []
    for i, at in every_device(sizes):
        out.append((i, index_of(partner(at), sizes)))
    return out


def pair_table(sizes, chunk, stage):
    n = dict(zip(AXES, sizes))

    def partner(at):
        axis, kind = ROUTES[chunk][at["head"]][stage]
        return {**at, axis: across(at[axis], kind, n[axis])}

    return pairs(sizes, partner)


def quad_tables(sizes, chunk):
    n = dict(zip(AXES, sizes))

    def partner(at, steps):
        for step in steps:
            axis, kind = ROUTES[chunk][at["head"]][step]
            at = {**at, axis: across(at[axis], kind, n[axis])}
        return at

    return [pairs(sizes, lambda at, steps=steps: partner(at, steps)) for steps in ((3,), (2,), (2, 3))]


def x_tables(sizes):
    n = dict(zip(AXES, sizes))

    def partner(at, kinds):
        x = at["seq"] * n["xl"] + at["xl"]
        for kind in kinds:
            x = across(x, kind, n["seq"] * n["xl"])
        return {**at, "seq": x // n["xl"], "xl": x % n["xl"]}

    return [pairs(sizes, lambda at, kinds=kinds: partner(at, kinds)) for kinds in ((0,), (1,), (0, 1))]


def z_table(sizes):
    n = sizes[AXES.index("z")]
    return pairs(sizes, lambda at: {**at, "z": (at["z"] + n // 2) % n})


def mask_of(chunk, head):
    masks = []
    for core in (0, 1):
        mask = jnp.int32(0)
        for axis, kind in ROUTES[chunk][core]:
            mask = mask * 2 + bit_of(lax.axis_index(axis).astype(jnp.int32), kind)
        masks.append(mask)
    return jnp.where(head == 0, masks[0], masks[1])


def add(*terms):
    terms = [t.astype(F32) for t in terms]
    while len(terms) > 1:
        terms = [sum(terms[i + 1 : i + 2], terms[i]) for i in range(0, len(terms), 2)]
    return terms[0].astype(BF)


def place_call(masks, upper, scale, parts, shape, before=None):
    _, piece, width = parts[0].shape
    spec = pl.BlockSpec((4 * piece, width), lambda c, b, s: (2 * ((s[c] >> 3) ^ upper) + b, c))
    held = pl.BlockSpec(parts[0].shape, lambda c, b, s: (0, 0, 0))
    args, specs, alias = list(parts), [held] * 4, None
    if before is not None:
        args, specs, alias = args + [before], specs + [pl.BlockSpec(memory_space=pl.ANY)], {5: 0}
    return call(
        functools.partial(place_kernel, scale=scale, upper=upper), masks, (2, 2), specs, spec,
        jax.ShapeDtypeStruct(shape, F32), [], 10**6, 4 * 10**6, args, alias,
    )


def reduce_grad(turned, cot, scale, head):
    share, width = turned.shape[0], cot.shape[1]
    sizes = tuple(lax.axis_size(a) for a in AXES)
    masks = [mask_of(c, head) for c in range(2)]
    piece = share // 16
    four = jax.ShapeDtypeStruct((4, piece, width // 2), BF)
    move = lambda value, table: lax.ppermute(value, AXES, table)
    tables = [[pair_table(sizes, c, stage) for stage in range(2)] for c in range(2)]
    quads = [quad_tables(sizes, c) for c in range(2)]
    held = []
    for c in range(2):
        held.append(call(
            grad_kernel, masks[c][None], (1,),
            [whole(turned.shape), pl.BlockSpec((cot.shape[0], width // 2), lambda g, s, c=c: (0, c))],
            [whole(four.shape)] * 4, [four] * 4, [], 6 * 10**8, 4 * 10**6, (turned, cot),
        ))
    own = []
    for c in range(2):
        last, third, second, first = held[c]
        got_last = move(last, tables[c][0])
        got_third = move(third, tables[c][0])
        got = move(add(second, got_last), tables[c][1])
        at = lambda i: (first[i : i + 1], got_third[i : i + 1], got[i : i + 1])
        away = [move(add(*at(i)), quads[c][i - 1]) for i in (1, 2, 3)]
        own.append(add(add(*at(0)), *away))
    both = jnp.concatenate(own, axis=0)
    near, over, far = [move(both, table) for table in x_tables(sizes)]
    both = add(both, near, over, far)
    both = add(both, move(both, z_table(sizes)))
    lower, upper = [], []
    for c in range(2):
        mine = both[c : c + 1]
        four = jnp.concatenate([mine] + [move(mine, table) for table in quads[c]], axis=0)
        next_four = move(four, tables[c][1])
        lower += [four, next_four]
        upper += [move(four, tables[c][0]), move(next_four, tables[c][0])]
    masks = jnp.stack(masks)
    out = place_call(masks, 0, scale, lower, (share, width))
    return place_call(masks, 1, scale, upper, (share, width), out)


def body(tokens, lengths, owner_slot, latent_index, cotangent, qkv_weight, out_weight):
    own = tokens[0]
    rows, share = own.shape
    groups = share // GROUP
    seq = lax.axis_index("seq")
    head = lax.axis_index("head")
    place = jnp.stack([seq, head]).astype(jnp.int32)

    oth = swap(own, "head")
    foreign_own = swap(own, "seq")

    sizes = lengths[0]
    images = sizes.shape[0]
    ends = jnp.cumsum(sizes, dtype=jnp.int32)
    starts = ends - sizes
    pad = lambda a: jnp.tile(jnp.pad(a, (0, HD - images)), 2)
    bounds = jnp.pad(jnp.stack([pad(starts), pad(ends)]), ((0, 6), (0, 0)))

    scratch = lambda r, qr, kr: [
        pltpu.VMEM((r, 2 * share), BF),
        pltpu.VMEM((qr, 128), BF),
        pltpu.VMEM((kr, 128), BF),
        pltpu.VMEM((GROUP, GROUP), BF),
    ]
    weight = lambda j: pl.BlockSpec((1, 2 * share, GROUP), lambda g, s: (j, 0, g))
    q, acc = call(
        local_kernel, place, (groups,),
        [whole((8, 128)), whole((rows, share)), whole((rows, share)),
         pl.BlockSpec((3, 2 * share, GROUP), lambda g, s: (0, 0, g))],
        [columns(rows, GROUP), columns(rows, 2 * GROUP)],
        [jax.ShapeDtypeStruct((rows, share), BF), jax.ShapeDtypeStruct((rows, 2 * share), F32)],
        scratch(rows, rows, rows), 7 * 10**9, 12 * 10**6, (bounds, own, oth, qkv_weight), limit=FULL_VMEM,
    )
    foreign_own, q = lax.optimization_barrier((foreign_own, q))
    foreign_oth = swap(foreign_own, "head")
    attn, turned = call(
        foreign_kernel, place, (groups,),
        [whole((8, 128)), whole((rows, share)), whole((rows, share)), weight(1), weight(2),
         columns(rows, GROUP), columns(rows, 2 * GROUP)],
        [columns(rows, GROUP), pl.BlockSpec((GROUP, rows), lambda g, s: (g, 0))],
        [jax.ShapeDtypeStruct((rows, share), BF), jax.ShapeDtypeStruct((share, rows), BF)],
        scratch(rows, rows, rows)
        + [pltpu.VMEM((rows, GROUP), BF), pltpu.VMEM((rows, GROUP), BF), pltpu.VMEM((rows, 2 * GROUP), F32)],
        4 * 10**9, 14 * 10**6, (bounds, foreign_own, foreign_oth, qkv_weight, qkv_weight, q, acc), limit=FULL_VMEM,
    )
    count = 2 * rows * lax.axis_size("z") * lax.axis_size("y") * lax.axis_size("xl")
    grad_out = reduce_grad(turned, cotangent[0], count ** (-0.5), head)

    partial = call(
        send_kernel, place, (groups,),
        [whole((rows, share)), pl.BlockSpec((share, GROUP), lambda g, s: (0, (1 - s[1]) * groups + g))],
        columns(rows, GROUP), jax.ShapeDtypeStruct((rows, share), BF), [], 6 * 10**8, 3 * 10**6, (attn, out_weight),
    )
    recv = swap(partial, "head")

    slots = owner_slot[0]
    picks = starts[:, None] + jnp.remainder(latent_index[0], sizes[:, None])
    order = slots[None, :] == jnp.arange(images, dtype=jnp.int32)[:, None]
    by_slot = jnp.sum(jnp.where(order[:, :, None], picks[None], 0), axis=1).reshape(2, rows)
    local = by_slot - seq * rows
    local = jnp.stack([jnp.where(seq == 0, local[1], local[0]), jnp.where(seq == 0, local[0], local[1])])
    local = local.reshape(2 * rows, 1)

    shape = jax.ShapeDtypeStruct((rows, share), BF)
    mixed, send, keep = call(
        mixed_kernel, place, (groups,),
        [whole((rows, share)), pl.BlockSpec((share, GROUP), lambda g, s: (0, s[1] * groups + g)),
         columns(rows, GROUP), whole((2 * rows, 1))],
        [columns(rows, GROUP)] * 3, [shape] * 3, [], 14 * 10**8, 6 * 10**6, (attn, out_weight, recv, local),
    )
    latents = keep + swap(send, "seq")

    return mixed[None], latents[None], grad_out


def on_mesh(fine):
    dp = ("z", "y", "xl")
    in_specs = (
        P(dp, "seq", "head"),
        P(dp, None),
        P(dp, None),
        P(dp, None, None),
        P(dp, "seq", None),
        P(None, None, "head"),
        P("head", None),
    )
    out_specs = (P(dp, "seq", "head"), P(dp, "seq", "head"), P("head", None))
    return jax.shard_map(body, mesh=fine, in_specs=in_specs, out_specs=out_specs, check_vma=False)


def solution(mesh):
    return on_mesh(Mesh(mesh.devices.reshape(2, 2, 8, 4, 2), ("seq", "head", "z", "y", "xl")))
```

```python
import functools

import jax
import jax.numpy as jnp
from jax import lax
from jax.experimental import pallas as pl
from jax.experimental.pallas import tpu as pltpu
from jax.sharding import Mesh
from jax.sharding import PartitionSpec as P

HD = 64
LAT = 128
IMAGES = 8
HEADER = 4
GROUP = 256
BIG = 128.0
EPS_NORM = 1e-05
EPS_HEAD = 1e-06
BF = jnp.bfloat16
F32 = jnp.float32
VMEM_LIMIT = 20 * 1024 * 1024
FULL_VMEM = 60 * 1024 * 1024


def norm_rows(head, own_ref, oth_ref, normed_ref, rows):
    share = own_ref.shape[1]
    step = 64

    def one(i, carry):
        at = pl.ds(pl.multiple_of(i * step, step), step)
        own = own_ref[at, :].astype(F32)
        oth = oth_ref[at, :].astype(F32)
        inv = 1.0 / (2 * share)
        mean = (jnp.sum(own, axis=1, keepdims=True) + jnp.sum(oth, axis=1, keepdims=True)) * inv
        own = own - mean
        oth = oth - mean
        var = (jnp.sum(own * own, axis=1, keepdims=True) + jnp.sum(oth * oth, axis=1, keepdims=True)) * inv
        scale = lax.rsqrt(var + EPS_NORM)
        own = (own * scale).astype(BF)
        oth = (oth * scale).astype(BF)

        @pl.when(head == 0)
        def _():
            normed_ref[at, :share] = own
            normed_ref[at, share:] = oth

        @pl.when(head != 0)
        def _():
            normed_ref[at, :share] = oth
            normed_ref[at, share:] = own

        return carry

    lax.fori_loop(0, rows // step, one, 0)


def head_norm(values, ones):
    mean = jnp.dot((values * values).astype(BF), ones, preferred_element_type=F32)
    return values * lax.rsqrt(mean + EPS_HEAD)


def ones_block():
    row = lax.broadcasted_iota(jnp.int32, (GROUP, GROUP), 0) // HD
    col = lax.broadcasted_iota(jnp.int32, (GROUP, GROUP), 1) // HD
    return jnp.where(row == col, 1.0 / HD, 0.0).astype(BF)


def features(place_ref, first, rows, inside, constant):
    pos = first + lax.broadcasted_iota(jnp.int32, (rows, 128), 0)
    lane = lax.broadcasted_iota(jnp.int32, (1, 128), 1) & (HD - 1)
    starts = jnp.zeros((1, 128), jnp.int32)
    ends = jnp.zeros((1, 128), jnp.int32)
    end = jnp.int32(0)
    for i in range(IMAGES):
        starts = jnp.where(lane == i, end, starts)
        end = end + place_ref[HEADER + i]
        ends = jnp.where(lane == i, end, ends)
    member = (pos >= starts) & (pos < ends)
    return jnp.where(lane == IMAGES, constant, jnp.where(member, inside, 0.0)).astype(BF)


def lower_half(rows):
    return lax.broadcasted_iota(jnp.int32, (rows, 128), 1) < HD


def attend_group(q, k, v, qfeat, kfeat, emit):
    q = (q.astype(F32) * 0.125).astype(BF)
    for pair in range(2):
        lanes = slice(pair * 128, pair * 128 + 128)
        qp, kp, vp = q[:, lanes], k[:, lanes], v[:, lanes]
        qlow, klow = lower_half(qp.shape[0]), lower_half(kp.shape[0])
        one = jnp.ones_like(vp)
        for odd in range(2):
            qa = jnp.where(qlow, qfeat, qp) if odd else jnp.where(qlow, qp, qfeat)
            ka = jnp.where(klow, kfeat, kp) if odd else jnp.where(klow, kp, kfeat)
            va = jnp.where(klow, one, vp) if odd else jnp.where(klow, vp, one)
            s = lax.dot_general(qa, ka, (((1,), (1,)), ((), ())), preferred_element_type=F32)
            w = jnp.exp(s).astype(BF)
            emit(2 * pair + odd, jnp.dot(w, va, preferred_element_type=F32))


def local_kernel(place_ref, own_ref, oth_ref, w_ref, q_ref, acc_ref, normed_ref, qf_ref, kf_ref, ones_ref):
    rows = own_ref.shape[0]

    @pl.when(pl.program_id(0) == 0)
    def _():
        norm_rows(place_ref[1], own_ref, oth_ref, normed_ref, rows)
        first = place_ref[0] * rows
        qf_ref[...] = features(place_ref, first, rows, BIG, -BIG)
        kf_ref[...] = features(place_ref, first, rows, 1.0, 1.0)
        ones_ref[...] = ones_block()

    normed = normed_ref[...]
    ones = ones_ref[...]
    q = head_norm(jnp.dot(normed, w_ref[0], preferred_element_type=F32), ones).astype(BF)
    k = head_norm(jnp.dot(normed, w_ref[1], preferred_element_type=F32), ones).astype(BF)
    v = jnp.dot(normed, w_ref[2], preferred_element_type=F32).astype(BF)
    q_ref[...] = q

    def emit(head, r):
        acc_ref[:, head * 128 : head * 128 + 128] = r

    attend_group(q, k, v, qf_ref[...], kf_ref[...], emit)


def foreign_kernel(place_ref, own_ref, oth_ref, wk_ref, wv_ref, q_ref, acc_in_ref, attn_ref, t0_ref, t1_ref, t2_ref, t3_ref, normed_ref, qf_ref, kf_ref, ones_ref, k_ref, v_ref, acc_ref, turned_ref):
    rows = own_ref.shape[0]
    half = rows // 2

    @pl.when(pl.program_id(0) == 0)
    def _():
        norm_rows(place_ref[1], own_ref, oth_ref, normed_ref, rows)
        qf_ref[...] = features(place_ref, place_ref[0] * rows, rows, BIG, -BIG)
        kf_ref[...] = features(place_ref, (1 - place_ref[0]) * rows, rows, 1.0, 1.0)
        ones_ref[...] = ones_block()

    normed = normed_ref[...]
    k_ref[...] = head_norm(jnp.dot(normed, wk_ref[0], preferred_element_type=F32), ones_ref[...]).astype(BF)
    v_ref[...] = jnp.dot(normed, wv_ref[0], preferred_element_type=F32).astype(BF)
    near = pl.ds(pl.multiple_of(place_ref[0] * half, half), half)
    far = pl.ds(pl.multiple_of((1 - place_ref[0]) * half, half), half)

    def emit_near(head, r):
        lanes = slice(head * 128, head * 128 + 128)
        acc_ref[:, lanes] = acc_in_ref[:, lanes] + r

    attend_group(q_ref[...], k_ref[near, :], v_ref[near, :], qf_ref[...], kf_ref[near, :], emit_near)

    def emit_far(head, r):
        lanes = slice(head * 128, head * 128 + 128)
        acc_ref[far, lanes] = acc_ref[far, lanes] + r

    attend_group(q_ref[far, :], k_ref[far, :], v_ref[far, :], qf_ref[far, :], kf_ref[far, :], emit_far)
    low = lower_half(rows)
    for pair in range(2):
        even = acc_ref[:, pair * 256 : pair * 256 + 128]
        odd = acc_ref[:, pair * 256 + 128 : pair * 256 + 256]
        total = pltpu.roll(jnp.where(low, odd, even), HD, 1)
        attn_ref[:, pair * 128 : pair * 128 + 128] = (jnp.where(low, even, odd) / total).astype(BF)
    group = pl.program_id(0)
    turned_ref[pl.ds(pl.multiple_of(group * GROUP, GROUP), GROUP), :] = attn_ref[...].T

    @pl.when(group == pl.num_programs(0) - 1)
    def _():
        for i, out in enumerate((t0_ref, t1_ref, t2_ref, t3_ref)):
            part = out.shape[0]
            out[...] = turned_ref[pl.ds(pl.multiple_of((i ^ place_ref[2]) * part, part), part), :]


def send_kernel(place_ref, attn_ref, w_ref, out_ref):
    out_ref[...] = jnp.dot(attn_ref[...], w_ref[...], preferred_element_type=F32).astype(BF)


def mixed_kernel(place_ref, attn_ref, w_ref, recv_ref, pick_ref, mixed_ref, send_ref, keep_ref):
    rows = attn_ref.shape[0]
    mixed = (jnp.dot(attn_ref[...], w_ref[...], preferred_element_type=F32) + recv_ref[...].astype(F32)).astype(BF)
    mixed_ref[...] = mixed
    row = lax.broadcasted_iota(jnp.int32, (rows, rows), 1)
    for half, out in ((0, send_ref), (1, keep_ref)):
        hot = jnp.where(pick_ref[half * rows : half * rows + rows, :] == row, 1.0, 0.0).astype(BF)
        out[...] = jnp.dot(hot, mixed, preferred_element_type=F32).astype(BF)


def call(kernel, place, grid, in_specs, out_specs, out_shape, scratch, flops, nbytes, args, alias=None, limit=VMEM_LIMIT):
    return pl.pallas_call(
        kernel,
        grid_spec=pltpu.PrefetchScalarGridSpec(
            num_scalar_prefetch=1, grid=grid, in_specs=in_specs, out_specs=out_specs, scratch_shapes=scratch
        ),
        out_shape=out_shape,
        input_output_aliases=alias or {},
        cost_estimate=pl.CostEstimate(flops=flops, bytes_accessed=nbytes, transcendentals=0),
        compiler_params=pltpu.CompilerParams(vmem_limit_bytes=limit),
    )(place, *args)


def whole(shape):
    return pl.BlockSpec(shape, lambda g, s: (0,) * len(shape))


def columns(rows, width):
    return pl.BlockSpec((rows, width), lambda g, s: (0, g))


def swap(value, axis):
    return lax.ppermute(value, axis, [(0, 1), (1, 0)])


def grad_kernel(place_ref, *refs):
    lefts, rights, outs, total_ref = refs[:4], refs[4:8], refs[8:12], refs[12]
    total = jnp.dot(lefts[0][...], rights[0][...], preferred_element_type=F32)
    for left, right in zip(lefts[1:], rights[1:]):
        total = total + jnp.dot(left[...], right[...], preferred_element_type=F32)
    total_ref[...] = total
    for i, out in enumerate(outs):
        piece = out.shape[0]
        out[...] = total_ref[pl.ds(pl.multiple_of((i ^ place_ref[3]) * piece, piece), piece), :].astype(BF)


def place_kernel(place_ref, part_ref, *refs, scale):
    out_ref = refs[-1]
    _, piece, _ = part_ref.shape
    for i in range(4):
        out_ref[i * piece : i * piece + piece, :] = part_ref[i ^ place_ref[3]].astype(F32) * scale


AXES = ("seq", "head", "z", "y", "xl")
ROUTES = (
    (("y", 0), ("y", 1), ("z", 0), ("z", 1)),
    (("z", 0), ("z", 1), ("y", 0), ("y", 1)),
)


def across(i, kind, n):
    if kind == 0:
        return i ^ 1
    return (i + 1) % n if i % 2 else (i - 1) % n


def bit_of(i, kind):
    return ((i + 1) >> 1) & 1 if kind == 0 else (i >> 1) & 1


def every_device(sizes):
    for i in range(sizes[0] * sizes[1] * sizes[2] * sizes[3] * sizes[4]):
        at, rest = {}, i
        for name, n in reversed(list(zip(AXES, sizes))):
            at[name] = rest % n
            rest //= n
        yield i, at


def index_of(at, sizes):
    i = 0
    for name, n in zip(AXES, sizes):
        i = i * n + at[name]
    return i


def pairs(sizes, partner):
    out = []
    for i, at in every_device(sizes):
        out.append((i, index_of(partner(at), sizes)))
    return out


def quad_tables(sizes, group):
    n = dict(zip(AXES, sizes))

    def partner(at, steps):
        for step in steps:
            axis, kind = ROUTES[at["head"]][2 * group + step]
            at = {**at, axis: across(at[axis], kind, n[axis])}
        return at

    return [pairs(sizes, lambda at, steps=steps: partner(at, steps)) for steps in ((1,), (0,), (0, 1))]


def x_tables(sizes):
    n = dict(zip(AXES, sizes))

    def partner(at, kinds):
        x = at["seq"] * n["xl"] + at["xl"]
        for kind in kinds:
            x = across(x, kind, n["seq"] * n["xl"])
        return {**at, "seq": x // n["xl"], "xl": x % n["xl"]}

    return [pairs(sizes, lambda at, kinds=kinds: partner(at, kinds)) for kinds in ((0,), (1,), (0, 1))]


def z_table(sizes):
    n = sizes[AXES.index("z")]
    return pairs(sizes, lambda at: {**at, "z": (at["z"] + n // 2) % n})


def mask_of(group, head):
    masks = []
    for core in (0, 1):
        mask = jnp.int32(0)
        for axis, kind in ROUTES[core][2 * group : 2 * group + 2]:
            mask = mask * 2 + bit_of(lax.axis_index(axis).astype(jnp.int32), kind)
        masks.append(mask)
    return jnp.where(head == 0, masks[0], masks[1])


def add(*terms):
    terms = [t.astype(F32) for t in terms]
    while len(terms) > 1:
        terms = [sum(terms[i + 1 : i + 2], terms[i]) for i in range(0, len(terms), 2)]
    return terms[0].astype(BF)


def move(value, table):
    return lax.ppermute(value, AXES, table)


def place_call(place, at, scale, part, before):
    _, piece, width = part.shape
    args, specs, alias = [part], [whole(part.shape)], None
    if before is not None:
        args, specs, alias = args + [before], specs + [pl.BlockSpec(memory_space=pl.ANY)], {2: 0}
    return call(
        functools.partial(place_kernel, scale=scale), place, (1,), specs,
        pl.BlockSpec((4 * piece, width), lambda g, s: (at ^ s[2], 0)),
        jax.ShapeDtypeStruct((16 * piece, width), F32), [], 10**6, 2 * 10**6, args, alias,
    )


def grad_call(place, lefts, rights):
    part, rows = lefts[0].shape
    width = rights[0].shape[1]
    piece = part // 4
    return call(
        grad_kernel, place, (width // GROUP,),
        [whole(lefts[0].shape)] * 4 + [columns(rows, GROUP)] * 4, [columns(piece, GROUP)] * 4,
        [jax.ShapeDtypeStruct((piece, width), BF)] * 4, [pltpu.VMEM((part, GROUP), F32)],
        12 * 10**8, 8 * 10**6, (*lefts, *rights),
    )


def body(tokens, lengths, owner_slot, latent_index, cotangent, qkv_weight, out_weight):
    own = tokens[0]
    rows, share = own.shape
    groups = share // GROUP
    seq = lax.axis_index("seq")
    head = lax.axis_index("head")
    sizes = lengths[0]
    ends = jnp.cumsum(sizes, dtype=jnp.int32)
    starts = ends - sizes
    place = jnp.concatenate([jnp.stack([seq, head, mask_of(0, head), mask_of(1, head)]).astype(jnp.int32), sizes])

    oth = swap(own, "head")
    foreign_own = swap(own, "seq")
    devices = tuple(lax.axis_size(a) for a in AXES)
    first, second = quad_tables(devices, 0), quad_tables(devices, 1)
    cots = [cotangent[0]] + [move(cotangent[0], table) for table in first]

    slots = owner_slot[0]
    picks = starts[:, None] + jnp.remainder(latent_index[0], sizes[:, None])
    order = slots[None, :] == jnp.arange(IMAGES, dtype=jnp.int32)[:, None]
    by_slot = jnp.sum(jnp.where(order[:, :, None], picks[None], 0), axis=1).reshape(2, rows)
    local = by_slot - seq * rows
    local = jnp.stack([jnp.where(seq == 0, local[1], local[0]), jnp.where(seq == 0, local[0], local[1])])
    local = local.reshape(2 * rows, 1)

    scratch = lambda r, qr, kr: [
        pltpu.VMEM((r, 2 * share), BF),
        pltpu.VMEM((qr, 128), BF),
        pltpu.VMEM((kr, 128), BF),
        pltpu.VMEM((GROUP, GROUP), BF),
    ]
    weight = lambda j: pl.BlockSpec((1, 2 * share, GROUP), lambda g, s: (j, 0, g))
    q, acc = call(
        local_kernel, place, (groups,),
        [whole((rows, share)), whole((rows, share)),
         pl.BlockSpec((3, 2 * share, GROUP), lambda g, s: (0, 0, g))],
        [columns(rows, GROUP), columns(rows, 2 * GROUP)],
        [jax.ShapeDtypeStruct((rows, share), BF), jax.ShapeDtypeStruct((rows, 2 * share), F32)],
        scratch(rows, rows, rows), 7 * 10**9, 12 * 10**6, (own, oth, qkv_weight), limit=FULL_VMEM,
    )
    foreign_own, q, local = lax.optimization_barrier((foreign_own, q, local))
    foreign_oth = swap(foreign_own, "head")
    quarter = whole((share // 4, rows))
    attn, *turned = call(
        foreign_kernel, place, (groups,),
        [whole((rows, share)), whole((rows, share)), weight(1), weight(2), columns(rows, GROUP), columns(rows, 2 * GROUP)],
        [columns(rows, GROUP)] + [quarter] * 4,
        [jax.ShapeDtypeStruct((rows, share), BF)] + [jax.ShapeDtypeStruct((share // 4, rows), BF)] * 4,
        scratch(rows, rows, rows)
        + [pltpu.VMEM((rows, GROUP), BF), pltpu.VMEM((rows, GROUP), BF), pltpu.VMEM((rows, 2 * GROUP), F32),
           pltpu.VMEM((share, rows), BF)],
        4 * 10**9, 14 * 10**6, (foreign_own, foreign_oth, qkv_weight, qkv_weight, q, acc), limit=FULL_VMEM,
    )
    lefts = [turned[0]] + [move(t, table) for t, table in zip(turned[1:], first)]

    partial = call(
        send_kernel, place, (groups,),
        [whole((rows, share)), pl.BlockSpec((share, GROUP), lambda g, s: (0, (1 - s[1]) * groups + g))],
        columns(rows, GROUP), jax.ShapeDtypeStruct((rows, share), BF), [], 6 * 10**8, 3 * 10**6, (attn, out_weight),
    )
    lefts[3], partial = lax.optimization_barrier((lefts[3], partial))
    recv = swap(partial, "head")

    pieces = grad_call(place, lefts, cots)
    grad = add(pieces[0], *[move(p, table) for p, table in zip(pieces[1:], second)])
    over_x = [move(grad, table) for table in x_tables(devices)]

    shape = jax.ShapeDtypeStruct((rows, share), BF)
    mixed, send, keep = call(
        mixed_kernel, place, (groups,),
        [whole((rows, share)), pl.BlockSpec((share, GROUP), lambda g, s: (0, s[1] * groups + g)),
         columns(rows, GROUP), whole((2 * rows, 1))],
        [columns(rows, GROUP)] * 3, [shape] * 3, [], 14 * 10**8, 6 * 10**6, (attn, out_weight, recv, local),
    )
    over_x[2], send = lax.optimization_barrier((over_x[2], send))
    grad = add(grad, *over_x)
    grad, send = lax.optimization_barrier((grad, send))
    latents = keep + swap(send, "seq")
    grad = add(grad, move(grad, z_table(devices)))
    held = jnp.stack([grad] + [move(grad, table) for table in second])
    held = [held] + [move(held, table) for table in first]
    scale = (2 * rows * lax.axis_size("z") * lax.axis_size("y") * lax.axis_size("xl")) ** (-0.5)
    grad_out = None
    for at, part in enumerate(held):
        grad_out = place_call(place, at, scale, part, grad_out)
    return mixed[None], latents[None], grad_out


def on_mesh(fine):
    dp = ("z", "y", "xl")
    in_specs = (
        P(dp, "seq", "head"),
        P(dp, None),
        P(dp, None),
        P(dp, None, None),
        P(dp, "seq", None),
        P(None, None, "head"),
        P("head", None),
    )
    out_specs = (P(dp, "seq", "head"), P(dp, "seq", "head"), P("head", None))
    return jax.shard_map(body, mesh=fine, in_specs=in_specs, out_specs=out_specs, check_vma=False)


def solution(mesh):
    return on_mesh(Mesh(mesh.devices.reshape(2, 2, 8, 4, 2), ("seq", "head", "z", "y", "xl")))
```

```python
import functools

import jax
import jax.numpy as jnp
from jax import lax
from jax.experimental import pallas as pl
from jax.experimental.pallas import tpu as pltpu
from jax.sharding import Mesh
from jax.sharding import PartitionSpec as P

HD = 64
LAT = 128
IMAGES = 8
HEADER = 4
GROUP = 256
BIG = 128.0
EPS_NORM = 1e-05
EPS_HEAD = 1e-06
BF = jnp.bfloat16
F32 = jnp.float32
VMEM_LIMIT = 20 * 1024 * 1024
BIG_VMEM = 60 * 1024 * 1024


def norm_rows(head, own_ref, oth_ref, normed_ref):
    rows, share = own_ref.shape
    step = 128
    one = jnp.ones((share, 128), BF)
    row_sum = lambda a, b: jnp.dot(a, one, preferred_element_type=F32) + jnp.dot(b, one, preferred_element_type=F32)
    wide = lambda value: jnp.concatenate([value] * (share // 128), axis=1)
    own_at = pl.ds(pl.multiple_of(head * share, share), share)
    oth_at = pl.ds(pl.multiple_of((1 - head) * share, share), share)
    for i in range(0, rows, step):
        at = slice(i, i + step)
        mean = wide(row_sum(own_ref[at, :], oth_ref[at, :]) * (0.5 / share))
        own = own_ref[at, :].astype(F32) - mean
        oth = oth_ref[at, :].astype(F32) - mean
        var = row_sum((own * own).astype(BF), (oth * oth).astype(BF)) * (0.5 / share)
        scale = wide(lax.rsqrt(var + EPS_NORM))
        normed_ref[at, own_at] = (own * scale).astype(BF)
        normed_ref[at, oth_at] = (oth * scale).astype(BF)


def head_norm(values, ones):
    mean = jnp.dot((values * values).astype(BF), ones, preferred_element_type=F32)
    return values * lax.rsqrt(mean + EPS_HEAD)


def ones_block():
    row = lax.broadcasted_iota(jnp.int32, (GROUP, GROUP), 0) >> 6
    col = lax.broadcasted_iota(jnp.int32, (GROUP, GROUP), 1) >> 6
    return jnp.where(row == col, 1.0 / HD, 0.0).astype(BF)


def features(place_ref, first, rows, inside, constant):
    pos = first + lax.broadcasted_iota(jnp.int32, (rows, 128), 0)
    lane = lax.broadcasted_iota(jnp.int32, (1, 128), 1) & (HD - 1)
    starts = jnp.zeros((1, 128), jnp.int32)
    ends = jnp.zeros((1, 128), jnp.int32)
    end = jnp.int32(0)
    for i in range(IMAGES):
        starts = jnp.where(lane == i, end, starts)
        end = end + place_ref[HEADER + i]
        ends = jnp.where(lane == i, end, ends)
    member = (pos >= starts) & (pos < ends)
    return jnp.where(lane == IMAGES, constant, jnp.where(member, inside, 0.0)).astype(BF)


def lower_half(rows):
    return lax.broadcasted_iota(jnp.int32, (rows, 128), 1) < HD


def attend_group(q, k, v, qfeat, kfeat, emit):
    for pair in range(2):
        lanes = slice(pair * 128, pair * 128 + 128)
        qp, kp, vp = (q(lanes).astype(F32) * 0.125).astype(BF), k(lanes), v(lanes)
        qlow, klow = lower_half(qp.shape[0]), lower_half(kp.shape[0])
        one = jnp.ones_like(vp)
        for odd in range(2):
            qa = jnp.where(qlow, qfeat, qp) if odd else jnp.where(qlow, qp, qfeat)
            ka = jnp.where(klow, kfeat, kp) if odd else jnp.where(klow, kp, kfeat)
            va = jnp.where(klow, one, vp) if odd else jnp.where(klow, vp, one)
            s = lax.dot_general(qa, ka, (((1,), (1,)), ((), ())), preferred_element_type=F32)
            w = jnp.exp(s).astype(BF)
            emit(2 * pair + odd, jnp.dot(w, va, preferred_element_type=F32))


def local_kernel(place_ref, own_ref, oth_ref, w_ref, q_ref, acc_ref, normed_ref, qf_ref, kf_ref, wbuf_ref, qbuf_ref, abuf_ref, k_ref, v_ref, sems):
    rows = own_ref.shape[0]
    groups = wbuf_ref.shape[0]
    loads = [
        pltpu.make_async_copy(w_ref.at[:, :, g * GROUP : g * GROUP + GROUP], wbuf_ref.at[g], sems.at[g])
        for g in range(groups)
    ]
    for load in loads:
        load.start()
    norm_rows(place_ref[1], own_ref, oth_ref, normed_ref)
    first = place_ref[0] * rows
    qf_ref[...] = features(place_ref, first, rows, BIG, -BIG)
    kf_ref[...] = features(place_ref, first, rows, 1.0, 1.0)
    ones = ones_block()
    stores = []
    for g in range(groups):
        loads[g].wait()
        normed = normed_ref[...]
        qbuf_ref[g] = head_norm(jnp.dot(normed, wbuf_ref[g, 0], preferred_element_type=F32), ones).astype(BF)
        k_ref[...] = head_norm(jnp.dot(normed, wbuf_ref[g, 1], preferred_element_type=F32), ones).astype(BF)
        v_ref[...] = jnp.dot(normed, wbuf_ref[g, 2], preferred_element_type=F32).astype(BF)
        stores.append(pltpu.make_async_copy(qbuf_ref.at[g], q_ref.at[g], sems.at[groups + g]))
        stores[-1].start()

        def emit(head, r):
            abuf_ref[g, :, head * 128 : head * 128 + 128] = r.astype(BF)

        attend_group(
            lambda lanes: qbuf_ref[g, :, lanes], lambda lanes: k_ref[:, lanes], lambda lanes: v_ref[:, lanes],
            qf_ref[...], kf_ref[...], emit,
        )
        stores.append(pltpu.make_async_copy(abuf_ref.at[g], acc_ref.at[g], sems.at[2 * groups + g]))
        stores[-1].start()
    for store in stores:
        store.wait()


def foreign_kernel(place_ref, own_ref, oth_ref, w_ref, q_ref, acc_ref, attn_ref, t0_ref, t1_ref, t2_ref, t3_ref, normed_ref, qf_ref, kf_ref, wbuf_ref, qbuf_ref, abuf_ref, k_ref, v_ref, sum_ref, turned_ref, sems):
    rows = own_ref.shape[0]
    half = rows // 2
    groups = wbuf_ref.shape[0]
    loads = []
    for g in range(groups):
        lanes = slice(g * GROUP, g * GROUP + GROUP)
        loads.append([
            pltpu.make_async_copy(w_ref.at[1:3, :, lanes], wbuf_ref.at[g], sems.at[g]),
            pltpu.make_async_copy(q_ref.at[g], qbuf_ref.at[g], sems.at[groups + g]),
            pltpu.make_async_copy(acc_ref.at[g], abuf_ref.at[g], sems.at[2 * groups + g]),
        ])
        for load in loads[-1]:
            load.start()
    norm_rows(place_ref[1], own_ref, oth_ref, normed_ref)
    qf_ref[...] = features(place_ref, place_ref[0] * rows, rows, BIG, -BIG)
    kf_ref[...] = features(place_ref, (1 - place_ref[0]) * rows, rows, 1.0, 1.0)
    ones = ones_block()
    near = pl.ds(pl.multiple_of(place_ref[0] * half, half), half)
    far = pl.ds(pl.multiple_of((1 - place_ref[0]) * half, half), half)
    low = lower_half(rows)
    for g in range(groups):
        for load in loads[g]:
            load.wait()
        normed = normed_ref[...]
        k_ref[...] = head_norm(jnp.dot(normed, wbuf_ref[g, 0], preferred_element_type=F32), ones).astype(BF)
        v_ref[...] = jnp.dot(normed, wbuf_ref[g, 1], preferred_element_type=F32).astype(BF)

        def emit_near(head, r):
            lanes = slice(head * 128, head * 128 + 128)
            sum_ref[:, lanes] = abuf_ref[g, :, lanes].astype(F32) + r

        def emit_far(head, r):
            lanes = slice(head * 128, head * 128 + 128)
            sum_ref[far, lanes] = sum_ref[far, lanes] + r

        attend_group(
            lambda lanes: qbuf_ref[g, :, lanes], lambda lanes: k_ref[near, lanes], lambda lanes: v_ref[near, lanes],
            qf_ref[...], kf_ref[near, :], emit_near,
        )
        attend_group(
            lambda lanes: qbuf_ref[g, far, lanes], lambda lanes: k_ref[far, lanes], lambda lanes: v_ref[far, lanes],
            qf_ref[far, :], kf_ref[far, :], emit_far,
        )
        for pair in range(2):
            even = sum_ref[:, pair * 256 : pair * 256 + 128]
            odd = sum_ref[:, pair * 256 + 128 : pair * 256 + 256]
            total = pltpu.roll(jnp.where(low, odd, even), HD, 1)
            first = g * GROUP + pair * 128
            attn = (jnp.where(low, even, odd) / total).astype(BF)
            attn_ref[:, first : first + 128] = attn
            turned_ref[first : first + 128, :] = attn.T
    for i, out in enumerate((t0_ref, t1_ref, t2_ref, t3_ref)):
        part = out.shape[0]
        out[...] = turned_ref[pl.ds(pl.multiple_of((i ^ place_ref[2]) * part, part), part), :]


def send_kernel(place_ref, attn_ref, w_ref, out_ref):
    out_ref[...] = jnp.dot(attn_ref[...], w_ref[...], preferred_element_type=F32).astype(BF)


def mixed_kernel(place_ref, attn_ref, w_ref, recv_ref, pick_ref, mixed_ref, send_ref, keep_ref):
    rows = attn_ref.shape[0]
    mixed = (jnp.dot(attn_ref[...], w_ref[...], preferred_element_type=F32) + recv_ref[...].astype(F32)).astype(BF)
    mixed_ref[...] = mixed
    row = lax.broadcasted_iota(jnp.int32, (rows, rows), 1)
    for half, out in ((0, send_ref), (1, keep_ref)):
        hot = jnp.where(pick_ref[half * rows : half * rows + rows, :] == row, 1.0, 0.0).astype(BF)
        out[...] = jnp.dot(hot, mixed, preferred_element_type=F32).astype(BF)


def call(kernel, place, grid, in_specs, out_specs, out_shape, scratch, flops, nbytes, args, alias=None, limit=VMEM_LIMIT):
    return pl.pallas_call(
        kernel,
        grid_spec=pltpu.PrefetchScalarGridSpec(
            num_scalar_prefetch=1, grid=grid, in_specs=in_specs, out_specs=out_specs, scratch_shapes=scratch
        ),
        out_shape=out_shape,
        input_output_aliases=alias or {},
        cost_estimate=pl.CostEstimate(flops=flops, bytes_accessed=nbytes, transcendentals=0),
        compiler_params=pltpu.CompilerParams(vmem_limit_bytes=limit),
    )(place, *args)


def whole(shape):
    return pl.BlockSpec(shape, lambda g, s: (0,) * len(shape))


def columns(rows, width):
    return pl.BlockSpec((rows, width), lambda g, s: (0, g))


def swap(value, axis):
    return lax.ppermute(value, axis, [(0, 1), (1, 0)])


def grad_kernel(place_ref, *refs):
    lefts, rights, outs, total_ref = refs[:4], refs[4:8], refs[8:12], refs[12]
    total = jnp.dot(lefts[0][...], rights[0][...], preferred_element_type=F32)
    for left, right in zip(lefts[1:], rights[1:]):
        total = total + jnp.dot(left[...], right[...], preferred_element_type=F32)
    total_ref[...] = total
    for i, out in enumerate(outs):
        piece = out.shape[0]
        out[...] = total_ref[pl.ds(pl.multiple_of((i ^ place_ref[3]) * piece, piece), piece), :].astype(BF)


def place_kernel(place_ref, part_ref, *refs, scale):
    out_ref = refs[-1]
    _, piece, _ = part_ref.shape
    for i in range(4):
        out_ref[i * piece : i * piece + piece, :] = part_ref[i ^ place_ref[3]].astype(F32) * scale


AXES = ("seq", "head", "z", "y", "xl")
ROUTES = (
    (("y", 0), ("y", 1), ("z", 0), ("z", 1)),
    (("z", 0), ("z", 1), ("y", 0), ("y", 1)),
)


def across(i, kind, n):
    if kind == 0:
        return i ^ 1
    return (i + 1) % n if i % 2 else (i - 1) % n


def bit_of(i, kind):
    return ((i + 1) >> 1) & 1 if kind == 0 else (i >> 1) & 1


def every_device(sizes):
    for i in range(sizes[0] * sizes[1] * sizes[2] * sizes[3] * sizes[4]):
        at, rest = {}, i
        for name, n in reversed(list(zip(AXES, sizes))):
            at[name] = rest % n
            rest //= n
        yield i, at


def index_of(at, sizes):
    i = 0
    for name, n in zip(AXES, sizes):
        i = i * n + at[name]
    return i


def pairs(sizes, partner):
    out = []
    for i, at in every_device(sizes):
        out.append((i, index_of(partner(at), sizes)))
    return out


def quad_tables(sizes, group):
    n = dict(zip(AXES, sizes))

    def partner(at, steps):
        for step in steps:
            axis, kind = ROUTES[at["head"]][2 * group + step]
            at = {**at, axis: across(at[axis], kind, n[axis])}
        return at

    return [pairs(sizes, lambda at, steps=steps: partner(at, steps)) for steps in ((1,), (0,), (0, 1))]


def x_tables(sizes):
    n = dict(zip(AXES, sizes))

    def partner(at, kinds):
        x = at["seq"] * n["xl"] + at["xl"]
        for kind in kinds:
            x = across(x, kind, n["seq"] * n["xl"])
        return {**at, "seq": x // n["xl"], "xl": x % n["xl"]}

    return [pairs(sizes, lambda at, kinds=kinds: partner(at, kinds)) for kinds in ((0,), (1,), (0, 1))]


def z_table(sizes):
    n = sizes[AXES.index("z")]
    return pairs(sizes, lambda at: {**at, "z": (at["z"] + n // 2) % n})


def mask_of(group, head):
    masks = []
    for core in (0, 1):
        mask = jnp.int32(0)
        for axis, kind in ROUTES[core][2 * group : 2 * group + 2]:
            mask = mask * 2 + bit_of(lax.axis_index(axis).astype(jnp.int32), kind)
        masks.append(mask)
    return jnp.where(head == 0, masks[0], masks[1])


def add(*terms):
    terms = [t.astype(F32) for t in terms]
    while len(terms) > 1:
        terms = [sum(terms[i + 1 : i + 2], terms[i]) for i in range(0, len(terms), 2)]
    return terms[0].astype(BF)


def move(value, table):
    return lax.ppermute(value, AXES, table)


def place_call(place, at, scale, part, before):
    _, piece, width = part.shape
    args, specs, alias = [part], [whole(part.shape)], None
    if before is not None:
        args, specs, alias = args + [before], specs + [pl.BlockSpec(memory_space=pl.ANY)], {2: 0}
    return call(
        functools.partial(place_kernel, scale=scale), place, (1,), specs,
        pl.BlockSpec((4 * piece, width), lambda g, s: (at ^ s[2], 0)),
        jax.ShapeDtypeStruct((16 * piece, width), F32), [], 10**6, 2 * 10**6, args, alias,
    )


def grad_call(place, lefts, rights):
    part, rows = lefts[0].shape
    width = rights[0].shape[1]
    piece = part // 4
    return call(
        grad_kernel, place, (width // GROUP,),
        [whole(lefts[0].shape)] * 4 + [columns(rows, GROUP)] * 4, [columns(piece, GROUP)] * 4,
        [jax.ShapeDtypeStruct((piece, width), BF)] * 4, [pltpu.VMEM((part, GROUP), F32)],
        12 * 10**8, 8 * 10**6, (*lefts, *rights),
    )


def body(tokens, lengths, owner_slot, latent_index, cotangent, qkv_weight, out_weight):
    own = tokens[0]
    rows, share = own.shape
    groups = share // GROUP
    seq = lax.axis_index("seq")
    head = lax.axis_index("head")
    sizes = lengths[0]
    place = jnp.concatenate([jnp.stack([seq, head, mask_of(0, head), mask_of(1, head)]).astype(jnp.int32), sizes])

    oth = swap(own, "head")
    foreign_own = swap(own, "seq")
    devices = tuple(lax.axis_size(a) for a in AXES)
    first, second = quad_tables(devices, 0), quad_tables(devices, 1)
    cots = [cotangent[0]] + [move(cotangent[0], table) for table in first]

    anywhere = pl.BlockSpec(memory_space=pl.ANY)
    scratch = lambda projections: [
        pltpu.VMEM((rows, 2 * share), BF),
        pltpu.VMEM((rows, 128), BF),
        pltpu.VMEM((rows, 128), BF),
        pltpu.VMEM((groups, projections, 2 * share, GROUP), BF),
        pltpu.VMEM((groups, rows, GROUP), BF),
        pltpu.VMEM((groups, rows, 2 * GROUP), BF),
        pltpu.VMEM((rows, GROUP), BF),
        pltpu.VMEM((rows, GROUP), BF),
    ]
    q, acc = call(
        local_kernel, place, (1,), [whole((rows, share)), whole((rows, share)), anywhere], [anywhere] * 2,
        [jax.ShapeDtypeStruct((groups, rows, GROUP), BF), jax.ShapeDtypeStruct((groups, rows, 2 * GROUP), BF)],
        scratch(3) + [pltpu.SemaphoreType.DMA((3 * groups,))], 10**8, 10**6, (own, oth, qkv_weight), limit=BIG_VMEM,
    )
    foreign_own, q, cots[1], cots[2] = lax.optimization_barrier((foreign_own, q, cots[1], cots[2]))
    foreign_oth = swap(foreign_own, "head")
    quarter = whole((share // 4, rows))
    attn, *turned = call(
        foreign_kernel, place, (1,), [whole((rows, share)), whole((rows, share))] + [anywhere] * 3,
        [whole((rows, share))] + [quarter] * 4,
        [jax.ShapeDtypeStruct((rows, share), BF)] + [jax.ShapeDtypeStruct((share // 4, rows), BF)] * 4,
        scratch(2)
        + [pltpu.VMEM((rows, 2 * GROUP), F32), pltpu.VMEM((share, rows), BF), pltpu.SemaphoreType.DMA((3 * groups,))],
        10**9, 10**6, (foreign_own, foreign_oth, qkv_weight, q, acc), limit=BIG_VMEM,
    )
    attn, latent_index, sizes, owner_slot = lax.optimization_barrier((attn, latent_index, sizes, owner_slot))
    ends = jnp.cumsum(sizes, dtype=jnp.int32)
    starts = ends - sizes
    slots = owner_slot[0]
    picks = starts[:, None] + jnp.remainder(latent_index[0], sizes[:, None])
    order = slots[None, :] == jnp.arange(IMAGES, dtype=jnp.int32)[:, None]
    by_slot = jnp.sum(jnp.where(order[:, :, None], picks[None], 0), axis=1).reshape(2, rows)
    local = by_slot - seq * rows
    local = jnp.stack([jnp.where(seq == 0, local[1], local[0]), jnp.where(seq == 0, local[0], local[1])])
    local = local.reshape(2 * rows, 1)

    lefts = [turned[0]] + [move(t, table) for t, table in zip(turned[1:], first)]

    partial = call(
        send_kernel, place, (groups,),
        [whole((rows, share)), pl.BlockSpec((share, GROUP), lambda g, s: (0, (1 - s[1]) * groups + g))],
        columns(rows, GROUP), jax.ShapeDtypeStruct((rows, share), BF), [], 6 * 10**8, 3 * 10**6, (attn, out_weight), limit=BIG_VMEM,
    )
    lefts[3], partial = lax.optimization_barrier((lefts[3], partial))
    recv = swap(partial, "head")

    pieces = grad_call(place, lefts, cots)
    grad = add(pieces[0], *[move(p, table) for p, table in zip(pieces[1:], second)])
    over_x = [move(grad, table) for table in x_tables(devices)]

    shape = jax.ShapeDtypeStruct((rows, share), BF)
    mixed, send, keep = call(
        mixed_kernel, place, (groups,),
        [whole((rows, share)), pl.BlockSpec((share, GROUP), lambda g, s: (0, s[1] * groups + g)),
         columns(rows, GROUP), whole((2 * rows, 1))],
        [columns(rows, GROUP)] * 3, [shape] * 3, [], 14 * 10**8, 6 * 10**6, (attn, out_weight, recv, local),
    )
    over_x[2], send = lax.optimization_barrier((over_x[2], send))
    grad = add(grad, *over_x)
    grad, send = lax.optimization_barrier((grad, send))
    latents = keep + swap(send, "seq")
    grad = add(grad, move(grad, z_table(devices)))
    held = jnp.stack([grad] + [move(grad, table) for table in second])
    held = [held] + [move(held, table) for table in first]
    scale = (2 * rows * lax.axis_size("z") * lax.axis_size("y") * lax.axis_size("xl")) ** (-0.5)
    grad_out = None
    for at, part in enumerate(held):
        grad_out = place_call(place, at, scale, part, grad_out)
    return mixed[None], latents[None], grad_out


def on_mesh(fine):
    dp = ("z", "y", "xl")
    in_specs = (
        P(dp, "seq", "head"),
        P(dp, None),
        P(dp, None),
        P(dp, None, None),
        P(dp, "seq", None),
        P(None, None, "head"),
        P("head", None),
    )
    out_specs = (P(dp, "seq", "head"), P(dp, "seq", "head"), P("head", None))
    return jax.shard_map(body, mesh=fine, in_specs=in_specs, out_specs=out_specs, check_vma=False)


def solution(mesh):
    return on_mesh(Mesh(mesh.devices.reshape(2, 2, 8, 4, 2), ("seq", "head", "z", "y", "xl")))
```

```python
import functools

import jax
import jax.numpy as jnp
from jax import lax
from jax.experimental import pallas as pl
from jax.experimental.pallas import tpu as pltpu
from jax.sharding import Mesh
from jax.sharding import PartitionSpec as P

HD = 64
LAT = 128
IMAGES = 8
HEADER = 4
GROUP = 256
BIG = 128.0
EPS_NORM = 1e-05
EPS_HEAD = 1e-06
BF = jnp.bfloat16
F32 = jnp.float32
VMEM_LIMIT = 20 * 1024 * 1024
BIG_VMEM = 60 * 1024 * 1024


def norm_rows(head, own_ref, oth_ref, normed_ref):
    rows, share = own_ref.shape
    step = 128
    one = jnp.ones((share, 128), BF)
    row_sum = lambda a, b: jnp.dot(a, one, preferred_element_type=F32) + jnp.dot(b, one, preferred_element_type=F32)
    wide = lambda value: jnp.concatenate([value] * (share // 128), axis=1)
    own_at = pl.ds(pl.multiple_of(head * share, share), share)
    oth_at = pl.ds(pl.multiple_of((1 - head) * share, share), share)
    for i in range(0, rows, step):
        at = slice(i, i + step)
        mean = wide(row_sum(own_ref[at, :], oth_ref[at, :]) * (0.5 / share))
        own = own_ref[at, :].astype(F32) - mean
        oth = oth_ref[at, :].astype(F32) - mean
        var = row_sum((own * own).astype(BF), (oth * oth).astype(BF)) * (0.5 / share)
        scale = wide(lax.rsqrt(var + EPS_NORM))
        normed_ref[at, own_at] = (own * scale).astype(BF)
        normed_ref[at, oth_at] = (oth * scale).astype(BF)


def head_norm(values, ones):
    mean = jnp.dot((values * values).astype(BF), ones, preferred_element_type=F32)
    return values * lax.rsqrt(mean + EPS_HEAD)


def ones_block():
    row = lax.broadcasted_iota(jnp.int32, (GROUP, GROUP), 0) >> 6
    col = lax.broadcasted_iota(jnp.int32, (GROUP, GROUP), 1) >> 6
    return jnp.where(row == col, 1.0 / HD, 0.0).astype(BF)


def features(place_ref, first, rows, inside, constant):
    pos = first + lax.broadcasted_iota(jnp.int32, (rows, 128), 0)
    lane = lax.broadcasted_iota(jnp.int32, (1, 128), 1) & (HD - 1)
    starts = jnp.zeros((1, 128), jnp.int32)
    ends = jnp.zeros((1, 128), jnp.int32)
    end = jnp.int32(0)
    for i in range(IMAGES):
        starts = jnp.where(lane == i, end, starts)
        end = end + place_ref[HEADER + i]
        ends = jnp.where(lane == i, end, ends)
    member = (pos >= starts) & (pos < ends)
    return jnp.where(lane == IMAGES, constant, jnp.where(member, inside, 0.0)).astype(BF)


def lower_half(rows):
    return lax.broadcasted_iota(jnp.int32, (rows, 128), 1) < HD


def attend_group(q, k, v, qfeat, kfeat, emit):
    for pair in range(2):
        lanes = slice(pair * 128, pair * 128 + 128)
        qp, kp, vp = (q(lanes).astype(F32) * 0.125).astype(BF), k(lanes), v(lanes)
        qlow, klow = lower_half(qp.shape[0]), lower_half(kp.shape[0])
        one = jnp.ones_like(vp)
        for odd in range(2):
            qa = jnp.where(qlow, qfeat, qp) if odd else jnp.where(qlow, qp, qfeat)
            ka = jnp.where(klow, kfeat, kp) if odd else jnp.where(klow, kp, kfeat)
            va = jnp.where(klow, one, vp) if odd else jnp.where(klow, vp, one)
            s = lax.dot_general(qa, ka, (((1,), (1,)), ((), ())), preferred_element_type=F32)
            w = jnp.exp(s).astype(BF)
            emit(2 * pair + odd, jnp.dot(w, va, preferred_element_type=F32))


def local_kernel(place_ref, own_ref, oth_ref, w_ref, q_ref, acc_ref, normed_ref, qf_ref, kf_ref, wbuf_ref, qbuf_ref, abuf_ref, k_ref, v_ref, sems):
    rows = own_ref.shape[0]
    groups = wbuf_ref.shape[0]
    loads = [
        pltpu.make_async_copy(w_ref.at[:, :, g * GROUP : g * GROUP + GROUP], wbuf_ref.at[g], sems.at[g])
        for g in range(groups)
    ]
    for load in loads:
        load.start()
    norm_rows(place_ref[1], own_ref, oth_ref, normed_ref)
    first = place_ref[0] * rows
    qf_ref[...] = features(place_ref, first, rows, BIG, -BIG)
    kf_ref[...] = features(place_ref, first, rows, 1.0, 1.0)
    ones = ones_block()
    stores = []
    for g in range(groups):
        loads[g].wait()
        normed = normed_ref[...]
        qbuf_ref[g] = head_norm(jnp.dot(normed, wbuf_ref[g, 0], preferred_element_type=F32), ones).astype(BF)
        k_ref[...] = head_norm(jnp.dot(normed, wbuf_ref[g, 1], preferred_element_type=F32), ones).astype(BF)
        v_ref[...] = jnp.dot(normed, wbuf_ref[g, 2], preferred_element_type=F32).astype(BF)
        stores.append(pltpu.make_async_copy(qbuf_ref.at[g], q_ref.at[g], sems.at[groups + g]))
        stores[-1].start()

        def emit(head, r):
            abuf_ref[g, :, head * 128 : head * 128 + 128] = r.astype(BF)

        attend_group(
            lambda lanes: qbuf_ref[g, :, lanes], lambda lanes: k_ref[:, lanes], lambda lanes: v_ref[:, lanes],
            qf_ref[...], kf_ref[...], emit,
        )
        stores.append(pltpu.make_async_copy(abuf_ref.at[g], acc_ref.at[g], sems.at[2 * groups + g]))
        stores[-1].start()
    for store in stores:
        store.wait()


def foreign_kernel(place_ref, own_ref, oth_ref, w_ref, q_ref, acc_ref, attn_ref, t0_ref, t1_ref, t2_ref, t3_ref, normed_ref, qf_ref, kf_ref, wbuf_ref, qbuf_ref, abuf_ref, k_ref, v_ref, sum_ref, turned_ref, sems):
    rows = own_ref.shape[0]
    half = rows // 2
    groups = wbuf_ref.shape[0]
    loads = []
    for g in range(groups):
        lanes = slice(g * GROUP, g * GROUP + GROUP)
        loads.append([
            pltpu.make_async_copy(w_ref.at[1:3, :, lanes], wbuf_ref.at[g], sems.at[g]),
            pltpu.make_async_copy(q_ref.at[g], qbuf_ref.at[g], sems.at[groups + g]),
            pltpu.make_async_copy(acc_ref.at[g], abuf_ref.at[g], sems.at[2 * groups + g]),
        ])
        for load in loads[-1]:
            load.start()
    norm_rows(place_ref[1], own_ref, oth_ref, normed_ref)
    qf_ref[...] = features(place_ref, place_ref[0] * rows, rows, BIG, -BIG)
    kf_ref[...] = features(place_ref, (1 - place_ref[0]) * rows, rows, 1.0, 1.0)
    ones = ones_block()
    near = pl.ds(pl.multiple_of(place_ref[0] * half, half), half)
    far = pl.ds(pl.multiple_of((1 - place_ref[0]) * half, half), half)
    low = lower_half(rows)
    for g in range(groups):
        for load in loads[g]:
            load.wait()
        normed = normed_ref[...]
        k_ref[...] = head_norm(jnp.dot(normed, wbuf_ref[g, 0], preferred_element_type=F32), ones).astype(BF)
        v_ref[...] = jnp.dot(normed, wbuf_ref[g, 1], preferred_element_type=F32).astype(BF)

        def emit_near(head, r):
            lanes = slice(head * 128, head * 128 + 128)
            sum_ref[:, lanes] = abuf_ref[g, :, lanes].astype(F32) + r

        def emit_far(head, r):
            lanes = slice(head * 128, head * 128 + 128)
            sum_ref[far, lanes] = sum_ref[far, lanes] + r

        attend_group(
            lambda lanes: qbuf_ref[g, :, lanes], lambda lanes: k_ref[near, lanes], lambda lanes: v_ref[near, lanes],
            qf_ref[...], kf_ref[near, :], emit_near,
        )
        attend_group(
            lambda lanes: qbuf_ref[g, far, lanes], lambda lanes: k_ref[far, lanes], lambda lanes: v_ref[far, lanes],
            qf_ref[far, :], kf_ref[far, :], emit_far,
        )
        for pair in range(2):
            even = sum_ref[:, pair * 256 : pair * 256 + 128]
            odd = sum_ref[:, pair * 256 + 128 : pair * 256 + 256]
            total = pltpu.roll(jnp.where(low, odd, even), HD, 1)
            first = g * GROUP + pair * 128
            attn = (jnp.where(low, even, odd) / total).astype(BF)
            attn_ref[:, first : first + 128] = attn
            turned_ref[first : first + 128, :] = attn.T
    for i, out in enumerate((t0_ref, t1_ref, t2_ref, t3_ref)):
        part = out.shape[0]
        out[...] = turned_ref[pl.ds(pl.multiple_of((i ^ place_ref[2]) * part, part), part), :]


def send_kernel(place_ref, attn_ref, w_ref, out_ref):
    out_ref[...] = jnp.dot(attn_ref[...], w_ref[...], preferred_element_type=F32).astype(BF)


def mixed_kernel(place_ref, attn_ref, w_ref, recv_ref, pick_ref, mixed_ref, send_ref, keep_ref):
    rows = attn_ref.shape[0]
    mixed = (jnp.dot(attn_ref[...], w_ref[...], preferred_element_type=F32) + recv_ref[...].astype(F32)).astype(BF)
    mixed_ref[...] = mixed
    row = lax.broadcasted_iota(jnp.int32, (rows, rows), 1)
    for half, out in ((0, send_ref), (1, keep_ref)):
        hot = jnp.where(pick_ref[half * rows : half * rows + rows, :] == row, 1.0, 0.0).astype(BF)
        out[...] = jnp.dot(hot, mixed, preferred_element_type=F32).astype(BF)


def call(kernel, place, grid, in_specs, out_specs, out_shape, scratch, flops, nbytes, args, alias=None, limit=VMEM_LIMIT):
    return pl.pallas_call(
        kernel,
        grid_spec=pltpu.PrefetchScalarGridSpec(
            num_scalar_prefetch=1, grid=grid, in_specs=in_specs, out_specs=out_specs, scratch_shapes=scratch
        ),
        out_shape=out_shape,
        input_output_aliases=alias or {},
        cost_estimate=pl.CostEstimate(flops=flops, bytes_accessed=nbytes, transcendentals=0),
        compiler_params=pltpu.CompilerParams(vmem_limit_bytes=limit),
    )(place, *args)


def whole(shape):
    return pl.BlockSpec(shape, lambda g, s: (0,) * len(shape))


def columns(rows, width):
    return pl.BlockSpec((rows, width), lambda g, s: (0, g))


def swap(value, axis):
    return lax.ppermute(value, axis, [(0, 1), (1, 0)])


def grad_kernel(place_ref, *refs):
    lefts, rights, outs, total_ref = refs[:4], refs[4:8], refs[8:12], refs[12]
    total = jnp.dot(lefts[0][...], rights[0][...], preferred_element_type=F32)
    for left, right in zip(lefts[1:], rights[1:]):
        total = total + jnp.dot(left[...], right[...], preferred_element_type=F32)
    total_ref[...] = total
    for i, out in enumerate(outs):
        piece = out.shape[0]
        out[...] = total_ref[pl.ds(pl.multiple_of((i ^ place_ref[3]) * piece, piece), piece), :].astype(BF)


def place_kernel(place_ref, part_ref, *refs, scale):
    refs[-1][...] = part_ref[0].astype(F32) * scale


AXES = ("seq", "head", "z", "y", "xl")
ROUTES = (
    (("y", 0), ("y", 1), ("z", 0), ("z", 1)),
    (("z", 0), ("z", 1), ("y", 0), ("y", 1)),
)


def across(i, kind, n):
    if kind == 0:
        return i ^ 1
    return (i + 1) % n if i % 2 else (i - 1) % n


def bit_of(i, kind):
    return ((i + 1) >> 1) & 1 if kind == 0 else (i >> 1) & 1


def every_device(sizes):
    for i in range(sizes[0] * sizes[1] * sizes[2] * sizes[3] * sizes[4]):
        at, rest = {}, i
        for name, n in reversed(list(zip(AXES, sizes))):
            at[name] = rest % n
            rest //= n
        yield i, at


def index_of(at, sizes):
    i = 0
    for name, n in zip(AXES, sizes):
        i = i * n + at[name]
    return i


def pairs(sizes, partner):
    out = []
    for i, at in every_device(sizes):
        out.append((i, index_of(partner(at), sizes)))
    return out


def quad_tables(sizes, group):
    n = dict(zip(AXES, sizes))

    def partner(at, steps):
        for step in steps:
            axis, kind = ROUTES[at["head"]][2 * group + step]
            at = {**at, axis: across(at[axis], kind, n[axis])}
        return at

    return [pairs(sizes, lambda at, steps=steps: partner(at, steps)) for steps in ((1,), (0,), (0, 1))]


def x_tables(sizes):
    n = dict(zip(AXES, sizes))

    def partner(at, kinds):
        x = at["seq"] * n["xl"] + at["xl"]
        for kind in kinds:
            x = across(x, kind, n["seq"] * n["xl"])
        return {**at, "seq": x // n["xl"], "xl": x % n["xl"]}

    return [pairs(sizes, lambda at, kinds=kinds: partner(at, kinds)) for kinds in ((0,), (1,), (0, 1))]


def z_table(sizes):
    n = sizes[AXES.index("z")]
    return pairs(sizes, lambda at: {**at, "z": (at["z"] + n // 2) % n})


def mask_of(group, head):
    masks = []
    for core in (0, 1):
        mask = jnp.int32(0)
        for axis, kind in ROUTES[core][2 * group : 2 * group + 2]:
            mask = mask * 2 + bit_of(lax.axis_index(axis).astype(jnp.int32), kind)
        masks.append(mask)
    return jnp.where(head == 0, masks[0], masks[1])


def add(*terms):
    terms = [t.astype(F32) for t in terms]
    while len(terms) > 1:
        terms = [sum(terms[i + 1 : i + 2], terms[i]) for i in range(0, len(terms), 2)]
    return terms[0].astype(BF)


def move(value, table):
    return lax.ppermute(value, AXES, table)


def place_call(place, at, start, scale, part, before):
    count, piece, width = part.shape
    args, specs, alias = [part], [pl.BlockSpec((1, piece, width), lambda g, s: (g, 0, 0))], None
    if before is not None:
        args, specs, alias = args + [before], specs + [pl.BlockSpec(memory_space=pl.ANY)], {2: 0}
    return call(
        functools.partial(place_kernel, scale=scale), place, (count,), specs,
        pl.BlockSpec((piece, width), lambda g, s: ((at ^ s[2]) * 4 + ((start + g) ^ s[3]), 0)),
        jax.ShapeDtypeStruct((16 * piece, width), F32), [], 10**6, 2 * 10**6, args, alias,
    )


def grad_call(place, lefts, rights):
    part, rows = lefts[0].shape
    width = rights[0].shape[1]
    piece = part // 4
    return call(
        grad_kernel, place, (width // GROUP,),
        [whole(lefts[0].shape)] * 4 + [columns(rows, GROUP)] * 4, [columns(piece, GROUP)] * 4,
        [jax.ShapeDtypeStruct((piece, width), BF)] * 4, [pltpu.VMEM((part, GROUP), F32)],
        12 * 10**8, 8 * 10**6, (*lefts, *rights), limit=BIG_VMEM,
    )


def body(tokens, lengths, owner_slot, latent_index, cotangent, qkv_weight, out_weight):
    own = tokens[0]
    rows, share = own.shape
    groups = share // GROUP
    seq = lax.axis_index("seq")
    head = lax.axis_index("head")
    sizes = lengths[0]
    place = jnp.concatenate([jnp.stack([seq, head, mask_of(0, head), mask_of(1, head)]).astype(jnp.int32), sizes])

    oth = swap(own, "head")
    foreign_own = swap(own, "seq")
    devices = tuple(lax.axis_size(a) for a in AXES)
    first, second = quad_tables(devices, 0), quad_tables(devices, 1)
    cot, place = lax.optimization_barrier((cotangent[0], place))
    cots = [cot] + [move(cot, table) for table in first]

    anywhere = pl.BlockSpec(memory_space=pl.ANY)
    scratch = lambda projections: [
        pltpu.VMEM((rows, 2 * share), BF),
        pltpu.VMEM((rows, 128), BF),
        pltpu.VMEM((rows, 128), BF),
        pltpu.VMEM((groups, projections, 2 * share, GROUP), BF),
        pltpu.VMEM((groups, rows, GROUP), BF),
        pltpu.VMEM((groups, rows, 2 * GROUP), BF),
        pltpu.VMEM((rows, GROUP), BF),
        pltpu.VMEM((rows, GROUP), BF),
    ]
    q, acc = call(
        local_kernel, place, (1,), [whole((rows, share)), whole((rows, share)), anywhere], [anywhere] * 2,
        [jax.ShapeDtypeStruct((groups, rows, GROUP), BF), jax.ShapeDtypeStruct((groups, rows, 2 * GROUP), BF)],
        scratch(3) + [pltpu.SemaphoreType.DMA((3 * groups,))], 10**8, 10**6, (own, oth, qkv_weight), limit=BIG_VMEM,
    )
    foreign_own, q, cots[1], cots[2] = lax.optimization_barrier((foreign_own, q, cots[1], cots[2]))
    foreign_oth = swap(foreign_own, "head")
    quarter = whole((share // 4, rows))
    attn, *turned = call(
        foreign_kernel, place, (1,), [whole((rows, share)), whole((rows, share))] + [anywhere] * 3,
        [whole((rows, share))] + [quarter] * 4,
        [jax.ShapeDtypeStruct((rows, share), BF)] + [jax.ShapeDtypeStruct((share // 4, rows), BF)] * 4,
        scratch(2)
        + [pltpu.VMEM((rows, 2 * GROUP), F32), pltpu.VMEM((share, rows), BF), pltpu.SemaphoreType.DMA((3 * groups,))],
        10**9, 10**6, (foreign_own, foreign_oth, qkv_weight, q, acc), limit=BIG_VMEM,
    )
    attn, latent_index, sizes, owner_slot = lax.optimization_barrier((attn, latent_index, sizes, owner_slot))
    ends = jnp.cumsum(sizes, dtype=jnp.int32)
    starts = ends - sizes
    slots = owner_slot[0]
    picks = starts[:, None] + jnp.remainder(latent_index[0], sizes[:, None])
    order = slots[None, :] == jnp.arange(IMAGES, dtype=jnp.int32)[:, None]
    by_slot = jnp.sum(jnp.where(order[:, :, None], picks[None], 0), axis=1).reshape(2, rows)
    local = by_slot - seq * rows
    local = jnp.stack([jnp.where(seq == 0, local[1], local[0]), jnp.where(seq == 0, local[0], local[1])])
    local = local.reshape(2 * rows, 1)

    lefts = [turned[0]] + [move(t, table) for t, table in zip(turned[1:], first)]

    partial = call(
        send_kernel, place, (groups,),
        [whole((rows, share)), pl.BlockSpec((share, GROUP), lambda g, s: (0, (1 - s[1]) * groups + g))],
        columns(rows, GROUP), jax.ShapeDtypeStruct((rows, share), BF), [], 6 * 10**8, 3 * 10**6, (attn, out_weight), limit=BIG_VMEM,
    )
    lefts[3], partial = lax.optimization_barrier((lefts[3], partial))
    recv = swap(partial, "head")

    pieces = grad_call(place, lefts, cots)
    grad = add(pieces[0], *[move(p, table) for p, table in zip(pieces[1:], second)])
    over_x = [move(grad, table) for table in x_tables(devices)]

    grad, attn = lax.optimization_barrier((add(grad, *over_x), attn))
    over_z = move(grad, z_table(devices))
    shape = jax.ShapeDtypeStruct((rows, share), BF)
    mixed, send, keep = call(
        mixed_kernel, place, (groups,),
        [whole((rows, share)), pl.BlockSpec((share, GROUP), lambda g, s: (0, s[1] * groups + g)),
         columns(rows, GROUP), whole((2 * rows, 1))],
        [columns(rows, GROUP)] * 3, [shape] * 3, [], 14 * 10**8, 6 * 10**6, (attn, out_weight, recv, local),
    )
    over_z, send = lax.optimization_barrier((over_z, send))
    grad = add(grad, over_z)
    latents = keep + swap(send, "seq")
    held = jnp.stack([grad] + [move(grad, table) for table in second])
    across_one, across_zero = move(held, first[0]), move(held, first[1])
    fourth = [move(across_one[:2], first[1]), move(across_zero[2:], first[0])]
    parts = [(0, 0, held), (1, 0, across_one), (2, 0, across_zero), (3, 0, fourth[0]), (3, 2, fourth[1])]
    scale = (2 * rows * lax.axis_size("z") * lax.axis_size("y") * lax.axis_size("xl")) ** (-0.5)
    grad_out = None
    for at, start, part in parts:
        grad_out = place_call(place, at, start, scale, part, grad_out)
    return mixed[None], latents[None], grad_out


def on_mesh(fine):
    dp = ("z", "y", "xl")
    in_specs = (
        P(dp, "seq", "head"),
        P(dp, None),
        P(dp, None),
        P(dp, None, None),
        P(dp, "seq", None),
        P(None, None, "head"),
        P("head", None),
    )
    out_specs = (P(dp, "seq", "head"), P(dp, "seq", "head"), P("head", None))
    return jax.shard_map(body, mesh=fine, in_specs=in_specs, out_specs=out_specs, check_vma=False)


def solution(mesh):
    return on_mesh(Mesh(mesh.devices.reshape(2, 2, 8, 4, 2), ("seq", "head", "z", "y", "xl")))
```

```python
import functools

import jax
import jax.numpy as jnp
from jax import lax
from jax.experimental import pallas as pl
from jax.experimental.pallas import tpu as pltpu
from jax.sharding import Mesh
from jax.sharding import PartitionSpec as P

HD = 64
LAT = 128
IMAGES = 8
HEADER = 4
GROUP = 256
BIG = 128.0
EPS_NORM = 1e-05
EPS_HEAD = 1e-06
BF = jnp.bfloat16
F32 = jnp.float32
VMEM_LIMIT = 20 * 1024 * 1024
BIG_VMEM = 60 * 1024 * 1024


def norm_rows(head, own_ref, oth_ref, normed_ref):
    rows, share = own_ref.shape
    step = 128
    one = jnp.ones((share, 128), BF)
    row_sum = lambda a, b: jnp.dot(a, one, preferred_element_type=F32) + jnp.dot(b, one, preferred_element_type=F32)
    wide = lambda value: jnp.concatenate([value] * (share // 128), axis=1)
    own_at = pl.ds(pl.multiple_of(head * share, share), share)
    oth_at = pl.ds(pl.multiple_of((1 - head) * share, share), share)
    for i in range(0, rows, step):
        at = slice(i, i + step)
        mean = wide(row_sum(own_ref[at, :], oth_ref[at, :]) * (0.5 / share))
        own = own_ref[at, :].astype(F32) - mean
        oth = oth_ref[at, :].astype(F32) - mean
        var = row_sum((own * own).astype(BF), (oth * oth).astype(BF)) * (0.5 / share)
        scale = wide(lax.rsqrt(var + EPS_NORM))
        normed_ref[at, own_at] = (own * scale).astype(BF)
        normed_ref[at, oth_at] = (oth * scale).astype(BF)


def head_norm(values, ones):
    mean = jnp.dot((values * values).astype(BF), ones, preferred_element_type=F32)
    return values * lax.rsqrt(mean + EPS_HEAD)


def ones_block():
    row = lax.broadcasted_iota(jnp.int32, (GROUP, GROUP), 0) >> 6
    col = lax.broadcasted_iota(jnp.int32, (GROUP, GROUP), 1) >> 6
    return jnp.where(row == col, 1.0 / HD, 0.0).astype(BF)


def features(place_ref, first, rows, inside, constant):
    pos = first + lax.broadcasted_iota(jnp.int32, (rows, 128), 0)
    lane = lax.broadcasted_iota(jnp.int32, (1, 128), 1) & (HD - 1)
    starts = jnp.zeros((1, 128), jnp.int32)
    ends = jnp.zeros((1, 128), jnp.int32)
    end = jnp.int32(0)
    for i in range(IMAGES):
        starts = jnp.where(lane == i, end, starts)
        end = end + place_ref[HEADER + i]
        ends = jnp.where(lane == i, end, ends)
    member = (pos >= starts) & (pos < ends)
    return jnp.where(lane == IMAGES, constant, jnp.where(member, inside, 0.0)).astype(BF)


def lower_half(rows):
    return lax.broadcasted_iota(jnp.int32, (rows, 128), 1) < HD


def attend_group(q, k, v, qfeat, kfeat, emit):
    for pair in range(2):
        lanes = slice(pair * 128, pair * 128 + 128)
        qp, kp, vp = (q(lanes).astype(F32) * 0.125).astype(BF), k(lanes), v(lanes)
        qlow, klow = lower_half(qp.shape[0]), lower_half(kp.shape[0])
        one = jnp.ones_like(vp)
        for odd in range(2):
            qa = jnp.where(qlow, qfeat, qp) if odd else jnp.where(qlow, qp, qfeat)
            ka = jnp.where(klow, kfeat, kp) if odd else jnp.where(klow, kp, kfeat)
            va = jnp.where(klow, one, vp) if odd else jnp.where(klow, vp, one)
            s = lax.dot_general(qa, ka, (((1,), (1,)), ((), ())), preferred_element_type=F32)
            w = jnp.exp(s).astype(BF)
            emit(2 * pair + odd, jnp.dot(w, va, preferred_element_type=F32))


def local_kernel(place_ref, own_ref, oth_ref, w_ref, q_ref, acc_ref, normed_ref, qf_ref, kf_ref, wbuf_ref, qbuf_ref, abuf_ref, k_ref, v_ref, sems):
    rows = own_ref.shape[0]
    groups = wbuf_ref.shape[0]
    loads = [
        pltpu.make_async_copy(w_ref.at[:, :, g * GROUP : g * GROUP + GROUP], wbuf_ref.at[g], sems.at[g])
        for g in range(groups)
    ]
    for load in loads:
        load.start()
    norm_rows(place_ref[1], own_ref, oth_ref, normed_ref)
    first = place_ref[0] * rows
    qf_ref[...] = features(place_ref, first, rows, BIG, -BIG)
    kf_ref[...] = features(place_ref, first, rows, 1.0, 1.0)
    ones = ones_block()
    stores = []
    for g in range(groups):
        loads[g].wait()
        normed = normed_ref[...]
        qbuf_ref[g] = head_norm(jnp.dot(normed, wbuf_ref[g, 0], preferred_element_type=F32), ones).astype(BF)
        k_ref[...] = head_norm(jnp.dot(normed, wbuf_ref[g, 1], preferred_element_type=F32), ones).astype(BF)
        v_ref[...] = jnp.dot(normed, wbuf_ref[g, 2], preferred_element_type=F32).astype(BF)
        stores.append(pltpu.make_async_copy(qbuf_ref.at[g], q_ref.at[g], sems.at[groups + g]))
        stores[-1].start()

        def emit(head, r):
            abuf_ref[g, :, head * 128 : head * 128 + 128] = r.astype(BF)

        attend_group(
            lambda lanes: qbuf_ref[g, :, lanes], lambda lanes: k_ref[:, lanes], lambda lanes: v_ref[:, lanes],
            qf_ref[...], kf_ref[...], emit,
        )
        stores.append(pltpu.make_async_copy(abuf_ref.at[g], acc_ref.at[g], sems.at[2 * groups + g]))
        stores[-1].start()
    for store in stores:
        store.wait()


def foreign_kernel(place_ref, own_ref, oth_ref, w_ref, q_ref, acc_ref, attn_ref, t0_ref, t1_ref, t2_ref, t3_ref, normed_ref, qf_ref, kf_ref, wbuf_ref, qbuf_ref, abuf_ref, k_ref, v_ref, sum_ref, turned_ref, sems):
    rows = own_ref.shape[0]
    half = rows // 2
    groups = wbuf_ref.shape[0]
    loads = []
    for g in range(groups):
        lanes = slice(g * GROUP, g * GROUP + GROUP)
        loads.append([
            pltpu.make_async_copy(w_ref.at[1:3, :, lanes], wbuf_ref.at[g], sems.at[g]),
            pltpu.make_async_copy(q_ref.at[g], qbuf_ref.at[g], sems.at[groups + g]),
            pltpu.make_async_copy(acc_ref.at[g], abuf_ref.at[g], sems.at[2 * groups + g]),
        ])
        for load in loads[-1]:
            load.start()
    norm_rows(place_ref[1], own_ref, oth_ref, normed_ref)
    qf_ref[...] = features(place_ref, place_ref[0] * rows, rows, BIG, -BIG)
    kf_ref[...] = features(place_ref, (1 - place_ref[0]) * rows, rows, 1.0, 1.0)
    ones = ones_block()
    near = pl.ds(pl.multiple_of(place_ref[0] * half, half), half)
    far = pl.ds(pl.multiple_of((1 - place_ref[0]) * half, half), half)
    low = lower_half(rows)
    for g in range(groups):
        for load in loads[g]:
            load.wait()
        normed = normed_ref[...]
        k_ref[...] = head_norm(jnp.dot(normed, wbuf_ref[g, 0], preferred_element_type=F32), ones).astype(BF)
        v_ref[...] = jnp.dot(normed, wbuf_ref[g, 1], preferred_element_type=F32).astype(BF)

        def emit_near(head, r):
            lanes = slice(head * 128, head * 128 + 128)
            sum_ref[:, lanes] = abuf_ref[g, :, lanes].astype(F32) + r

        def emit_far(head, r):
            lanes = slice(head * 128, head * 128 + 128)
            sum_ref[far, lanes] = sum_ref[far, lanes] + r

        attend_group(
            lambda lanes: qbuf_ref[g, :, lanes], lambda lanes: k_ref[near, lanes], lambda lanes: v_ref[near, lanes],
            qf_ref[...], kf_ref[near, :], emit_near,
        )
        attend_group(
            lambda lanes: qbuf_ref[g, far, lanes], lambda lanes: k_ref[far, lanes], lambda lanes: v_ref[far, lanes],
            qf_ref[far, :], kf_ref[far, :], emit_far,
        )
        for pair in range(2):
            even = sum_ref[:, pair * 256 : pair * 256 + 128]
            odd = sum_ref[:, pair * 256 + 128 : pair * 256 + 256]
            total = pltpu.roll(jnp.where(low, odd, even), HD, 1)
            first = g * GROUP + pair * 128
            attn = (jnp.where(low, even, odd) / total).astype(BF)
            attn_ref[:, first : first + 128] = attn
            turned_ref[first : first + 128, :] = attn.T
    for i, out in enumerate((t0_ref, t1_ref, t2_ref, t3_ref)):
        part = out.shape[0]
        out[...] = turned_ref[pl.ds(pl.multiple_of((i ^ place_ref[2]) * part, part), part), :]


def send_kernel(place_ref, attn_ref, w_ref, out_ref):
    out_ref[...] = jnp.dot(attn_ref[...], w_ref[...], preferred_element_type=F32).astype(BF)


def mixed_kernel(place_ref, attn_ref, w_ref, recv_ref, pick_ref, mixed_ref, send_ref, keep_ref):
    rows = attn_ref.shape[0]
    mixed = (jnp.dot(attn_ref[...], w_ref[...], preferred_element_type=F32) + recv_ref[...].astype(F32)).astype(BF)
    mixed_ref[...] = mixed
    row = lax.broadcasted_iota(jnp.int32, (rows, rows), 1)
    for half, out in ((0, send_ref), (1, keep_ref)):
        hot = jnp.where(pick_ref[half * rows : half * rows + rows, :] == row, 1.0, 0.0).astype(BF)
        out[...] = jnp.dot(hot, mixed, preferred_element_type=F32).astype(BF)


def call(kernel, place, grid, in_specs, out_specs, out_shape, scratch, flops, nbytes, args, alias=None, limit=VMEM_LIMIT):
    return pl.pallas_call(
        kernel,
        grid_spec=pltpu.PrefetchScalarGridSpec(
            num_scalar_prefetch=1, grid=grid, in_specs=in_specs, out_specs=out_specs, scratch_shapes=scratch
        ),
        out_shape=out_shape,
        input_output_aliases=alias or {},
        cost_estimate=pl.CostEstimate(flops=flops, bytes_accessed=nbytes, transcendentals=0),
        compiler_params=pltpu.CompilerParams(vmem_limit_bytes=limit),
    )(place, *args)


def whole(shape):
    return pl.BlockSpec(shape, lambda g, s: (0,) * len(shape))


def columns(rows, width):
    return pl.BlockSpec((rows, width), lambda g, s: (0, g))


def swap(value, axis):
    return lax.ppermute(value, axis, [(0, 1), (1, 0)])


def grad_kernel(place_ref, *refs):
    lefts, rights, outs, total_ref = refs[:4], refs[4:8], refs[8:12], refs[12]
    total = jnp.dot(lefts[0][...], rights[0][...], preferred_element_type=F32)
    for left, right in zip(lefts[1:], rights[1:]):
        total = total + jnp.dot(left[...], right[...], preferred_element_type=F32)
    total_ref[...] = total
    for i, out in enumerate(outs):
        piece = out.shape[0]
        out[...] = total_ref[pl.ds(pl.multiple_of((i ^ place_ref[3]) * piece, piece), piece), :].astype(BF)


def place_kernel(place_ref, *refs, count, scale):
    out_ref = refs[-1]
    for i in range(4):
        part_ref = refs[i * count // 4]
        of_each, piece, _ = part_ref.shape
        rows = pl.ds(pl.multiple_of((i ^ place_ref[3]) * piece, piece), piece)
        out_ref[rows, :] = part_ref[i % of_each].astype(F32) * scale


AXES = ("seq", "head", "z", "y", "xl")
ROUTES = (
    (("y", 0), ("y", 1), ("z", 0), ("z", 1)),
    (("z", 0), ("z", 1), ("y", 0), ("y", 1)),
)


def across(i, kind, n):
    if kind == 0:
        return i ^ 1
    return (i + 1) % n if i % 2 else (i - 1) % n


def bit_of(i, kind):
    return ((i + 1) >> 1) & 1 if kind == 0 else (i >> 1) & 1


def every_device(sizes):
    for i in range(sizes[0] * sizes[1] * sizes[2] * sizes[3] * sizes[4]):
        at, rest = {}, i
        for name, n in reversed(list(zip(AXES, sizes))):
            at[name] = rest % n
            rest //= n
        yield i, at


def index_of(at, sizes):
    i = 0
    for name, n in zip(AXES, sizes):
        i = i * n + at[name]
    return i


def pairs(sizes, partner):
    out = []
    for i, at in every_device(sizes):
        out.append((i, index_of(partner(at), sizes)))
    return out


def quad_tables(sizes, group):
    n = dict(zip(AXES, sizes))

    def partner(at, steps):
        for step in steps:
            axis, kind = ROUTES[at["head"]][2 * group + step]
            at = {**at, axis: across(at[axis], kind, n[axis])}
        return at

    return [pairs(sizes, lambda at, steps=steps: partner(at, steps)) for steps in ((1,), (0,), (0, 1))]


def x_tables(sizes):
    n = dict(zip(AXES, sizes))

    def partner(at, kinds):
        x = at["seq"] * n["xl"] + at["xl"]
        for kind in kinds:
            x = across(x, kind, n["seq"] * n["xl"])
        return {**at, "seq": x // n["xl"], "xl": x % n["xl"]}

    return [pairs(sizes, lambda at, kinds=kinds: partner(at, kinds)) for kinds in ((0,), (1,), (0, 1))]


def z_table(sizes):
    n = sizes[AXES.index("z")]
    return pairs(sizes, lambda at: {**at, "z": (at["z"] + n // 2) % n})


def mask_of(group, head):
    masks = []
    for core in (0, 1):
        mask = jnp.int32(0)
        for axis, kind in ROUTES[core][2 * group : 2 * group + 2]:
            mask = mask * 2 + bit_of(lax.axis_index(axis).astype(jnp.int32), kind)
        masks.append(mask)
    return jnp.where(head == 0, masks[0], masks[1])


def add(*terms):
    terms = [t.astype(F32) for t in terms]
    while len(terms) > 1:
        terms = [sum(terms[i + 1 : i + 2], terms[i]) for i in range(0, len(terms), 2)]
    return terms[0].astype(BF)


def move(value, table):
    return lax.ppermute(value, AXES, table)


def place_call(place, at, scale, parts, before):
    _, piece, width = parts[0].shape
    args, specs, alias = list(parts), [whole(part.shape) for part in parts], None
    if before is not None:
        args, specs, alias = args + [before], specs + [pl.BlockSpec(memory_space=pl.ANY)], {1 + len(parts): 0}
    return call(
        functools.partial(place_kernel, count=len(parts), scale=scale), place, (1,), specs,
        pl.BlockSpec((4 * piece, width), lambda g, s: (at ^ s[2], 0)),
        jax.ShapeDtypeStruct((16 * piece, width), F32), [], 10**6, 2 * 10**6, args, alias,
    )


def grad_call(place, lefts, rights):
    part, rows = lefts[0].shape
    width = rights[0].shape[1]
    piece = part // 4
    return call(
        grad_kernel, place, (width // GROUP,),
        [whole(lefts[0].shape)] * 4 + [columns(rows, GROUP)] * 4, [columns(piece, GROUP)] * 4,
        [jax.ShapeDtypeStruct((piece, width), BF)] * 4, [pltpu.VMEM((part, GROUP), F32)],
        12 * 10**8, 8 * 10**6, (*lefts, *rights), limit=BIG_VMEM,
    )


def body(tokens, lengths, owner_slot, latent_index, cotangent, qkv_weight, out_weight):
    own = tokens[0]
    rows, share = own.shape
    groups = share // GROUP
    seq = lax.axis_index("seq")
    head = lax.axis_index("head")
    sizes = lengths[0]
    place = jnp.concatenate([jnp.stack([seq, head, mask_of(0, head), mask_of(1, head)]).astype(jnp.int32), sizes])

    oth = swap(own, "head")
    foreign_own = swap(own, "seq")
    devices = tuple(lax.axis_size(a) for a in AXES)
    first, second = quad_tables(devices, 0), quad_tables(devices, 1)
    cots = [cotangent[0]] + [move(cotangent[0], table) for table in first]

    anywhere = pl.BlockSpec(memory_space=pl.ANY)
    scratch = lambda projections: [
        pltpu.VMEM((rows, 2 * share), BF),
        pltpu.VMEM((rows, 128), BF),
        pltpu.VMEM((rows, 128), BF),
        pltpu.VMEM((groups, projections, 2 * share, GROUP), BF),
        pltpu.VMEM((groups, rows, GROUP), BF),
        pltpu.VMEM((groups, rows, 2 * GROUP), BF),
        pltpu.VMEM((rows, GROUP), BF),
        pltpu.VMEM((rows, GROUP), BF),
    ]
    q, acc = call(
        local_kernel, place, (1,), [whole((rows, share)), whole((rows, share)), anywhere], [anywhere] * 2,
        [jax.ShapeDtypeStruct((groups, rows, GROUP), BF), jax.ShapeDtypeStruct((groups, rows, 2 * GROUP), BF)],
        scratch(3) + [pltpu.SemaphoreType.DMA((3 * groups,))], 10**8, 10**6, (own, oth, qkv_weight), limit=BIG_VMEM,
    )
    foreign_own, q, cots[1], cots[2] = lax.optimization_barrier((foreign_own, q, cots[1], cots[2]))
    foreign_oth = swap(foreign_own, "head")
    quarter = whole((share // 4, rows))
    attn, *turned = call(
        foreign_kernel, place, (1,), [whole((rows, share)), whole((rows, share))] + [anywhere] * 3,
        [whole((rows, share))] + [quarter] * 4,
        [jax.ShapeDtypeStruct((rows, share), BF)] + [jax.ShapeDtypeStruct((share // 4, rows), BF)] * 4,
        scratch(2)
        + [pltpu.VMEM((rows, 2 * GROUP), F32), pltpu.VMEM((share, rows), BF), pltpu.SemaphoreType.DMA((3 * groups,))],
        10**9, 10**6, (foreign_own, foreign_oth, qkv_weight, q, acc), limit=BIG_VMEM,
    )
    attn, latent_index, sizes, owner_slot = lax.optimization_barrier((attn, latent_index, sizes, owner_slot))
    ends = jnp.cumsum(sizes, dtype=jnp.int32)
    starts = ends - sizes
    slots = owner_slot[0]
    picks = starts[:, None] + jnp.remainder(latent_index[0], sizes[:, None])
    order = slots[None, :] == jnp.arange(IMAGES, dtype=jnp.int32)[:, None]
    by_slot = jnp.sum(jnp.where(order[:, :, None], picks[None], 0), axis=1).reshape(2, rows)
    local = by_slot - seq * rows
    local = jnp.stack([jnp.where(seq == 0, local[1], local[0]), jnp.where(seq == 0, local[0], local[1])])
    local = local.reshape(2 * rows, 1)

    lefts = [turned[0]] + [move(t, table) for t, table in zip(turned[1:], first)]

    pieces = list(grad_call(place, lefts, cots))
    pieces[0], attn = lax.optimization_barrier((pieces[0], attn))
    away = [move(p, table) for p, table in zip(pieces[1:], second)]
    partial = call(
        send_kernel, place, (groups,),
        [whole((rows, share)), pl.BlockSpec((share, GROUP), lambda g, s: (0, (1 - s[1]) * groups + g))],
        columns(rows, GROUP), jax.ShapeDtypeStruct((rows, share), BF), [], 6 * 10**8, 3 * 10**6, (attn, out_weight), limit=BIG_VMEM,
    )
    away[2], partial = lax.optimization_barrier((away[2], partial))
    grad = add(pieces[0], *away)
    recv = swap(partial, "head")
    over_x = [move(grad, table) for table in x_tables(devices)]
    over_x[2], local = lax.optimization_barrier((over_x[2], local))
    grad, attn = lax.optimization_barrier((add(grad, *over_x), attn))
    over_z = move(grad, z_table(devices))
    shape = jax.ShapeDtypeStruct((rows, share), BF)
    mixed, send, keep = call(
        mixed_kernel, place, (groups,),
        [whole((rows, share)), pl.BlockSpec((share, GROUP), lambda g, s: (0, s[1] * groups + g)),
         columns(rows, GROUP), whole((2 * rows, 1))],
        [columns(rows, GROUP)] * 3, [shape] * 3, [], 14 * 10**8, 6 * 10**6, (attn, out_weight, recv, local),
    )
    over_z, send = lax.optimization_barrier((over_z, send))
    grad = add(grad, over_z)
    latents = keep + swap(send, "seq")
    held = jnp.stack([grad] + [move(grad, table) for table in second])
    across_one, across_zero = move(held, first[0]), move(held, first[1])
    scale = (2 * rows * lax.axis_size("z") * lax.axis_size("y") * lax.axis_size("xl")) ** (-0.5)
    grad_out = place_call(place, 0, scale, [held], None)
    across_one, grad_out = lax.optimization_barrier((across_one, grad_out))
    fourth = [move(across_one[:2], first[1]), move(across_zero[2:], first[0])]
    grad_out = place_call(place, 1, scale, [across_one], grad_out)
    grad_out = place_call(place, 2, scale, [across_zero], grad_out)
    grad_out = place_call(place, 3, scale, fourth, grad_out)
    return mixed[None], latents[None], grad_out


def on_mesh(fine):
    dp = ("z", "y", "xl")
    in_specs = (
        P(dp, "seq", "head"),
        P(dp, None),
        P(dp, None),
        P(dp, None, None),
        P(dp, "seq", None),
        P(None, None, "head"),
        P("head", None),
    )
    out_specs = (P(dp, "seq", "head"), P(dp, "seq", "head"), P("head", None))
    return jax.shard_map(body, mesh=fine, in_specs=in_specs, out_specs=out_specs, check_vma=False)


def solution(mesh):
    return on_mesh(Mesh(mesh.devices.reshape(2, 2, 8, 4, 2), ("seq", "head", "z", "y", "xl")))
```

```python
import functools

import jax
import jax.numpy as jnp
from jax import lax
from jax.experimental import pallas as pl
from jax.experimental.pallas import tpu as pltpu
from jax.sharding import Mesh
from jax.sharding import PartitionSpec as P

HD = 64
LAT = 128
IMAGES = 8
HEADER = 4
GROUP = 256
BIG = 128.0
EPS_NORM = 1e-05
EPS_HEAD = 1e-06
BF = jnp.bfloat16
F32 = jnp.float32
VMEM_LIMIT = 20 * 1024 * 1024
BIG_VMEM = 60 * 1024 * 1024


def norm_rows(head, own_ref, oth_ref, normed_ref):
    rows, share = own_ref.shape
    step = 128
    one = jnp.ones((share, 128), BF)
    row_sum = lambda a, b: jnp.dot(a, one, preferred_element_type=F32) + jnp.dot(b, one, preferred_element_type=F32)
    wide = lambda value: jnp.concatenate([value] * (share // 128), axis=1)
    own_at = pl.ds(pl.multiple_of(head * share, share), share)
    oth_at = pl.ds(pl.multiple_of((1 - head) * share, share), share)
    def block(i, carry):
        at = pl.ds(pl.multiple_of(i * step, step), step)
        mean = wide(row_sum(own_ref[at, :], oth_ref[at, :]) * (0.5 / share))
        own = own_ref[at, :].astype(F32) - mean
        oth = oth_ref[at, :].astype(F32) - mean
        var = row_sum((own * own).astype(BF), (oth * oth).astype(BF)) * (0.5 / share)
        scale = wide(lax.rsqrt(var + EPS_NORM))
        normed_ref[at, own_at] = (own * scale).astype(BF)
        normed_ref[at, oth_at] = (oth * scale).astype(BF)
        return carry

    lax.fori_loop(0, rows // step, block, 0)


def head_norm(values, ones):
    mean = jnp.dot((values * values).astype(BF), ones, preferred_element_type=F32)
    return values * lax.rsqrt(mean + EPS_HEAD)


def ones_block():
    row = lax.broadcasted_iota(jnp.int32, (GROUP, GROUP), 0) >> 6
    col = lax.broadcasted_iota(jnp.int32, (GROUP, GROUP), 1) >> 6
    return jnp.where(row == col, 1.0 / HD, 0.0).astype(BF)


def features(place_ref, first, rows, inside, constant):
    pos = first + lax.broadcasted_iota(jnp.int32, (rows, 128), 0)
    lane = lax.broadcasted_iota(jnp.int32, (1, 128), 1) & (HD - 1)
    starts = jnp.zeros((1, 128), jnp.int32)
    ends = jnp.zeros((1, 128), jnp.int32)
    end = jnp.int32(0)
    for i in range(IMAGES):
        starts = jnp.where(lane == i, end, starts)
        end = end + place_ref[HEADER + i]
        ends = jnp.where(lane == i, end, ends)
    member = (pos >= starts) & (pos < ends)
    return jnp.where(lane == IMAGES, constant, jnp.where(member, inside, 0.0)).astype(BF)


def lower_half(rows):
    return lax.broadcasted_iota(jnp.int32, (rows, 128), 1) < HD


def attend_group(q, k, v, qfeat, kfeat, emit):
    for pair in range(2):
        lanes = slice(pair * 128, pair * 128 + 128)
        qp, kp, vp = (q(lanes).astype(F32) * 0.125).astype(BF), k(lanes), v(lanes)
        qlow, klow = lower_half(qp.shape[0]), lower_half(kp.shape[0])
        one = jnp.ones_like(vp)
        for odd in range(2):
            qa = jnp.where(qlow, qfeat, qp) if odd else jnp.where(qlow, qp, qfeat)
            ka = jnp.where(klow, kfeat, kp) if odd else jnp.where(klow, kp, kfeat)
            va = jnp.where(klow, one, vp) if odd else jnp.where(klow, vp, one)
            s = lax.dot_general(qa, ka, (((1,), (1,)), ((), ())), preferred_element_type=F32)
            w = jnp.exp(s).astype(BF)
            emit(2 * pair + odd, jnp.dot(w, va, preferred_element_type=F32))


def local_kernel(place_ref, own_ref, oth_ref, w_ref, q_ref, acc_ref, normed_ref, qf_ref, kf_ref, wbuf_ref, qbuf_ref, abuf_ref, k_ref, v_ref, sems):
    rows = own_ref.shape[0]
    groups = wbuf_ref.shape[0]

    def load(g):
        lanes = pl.ds(pl.multiple_of(g * GROUP, GROUP), GROUP)
        return pltpu.make_async_copy(w_ref.at[:, :, lanes], wbuf_ref.at[g], sems.at[g])

    def stores(g):
        return (
            pltpu.make_async_copy(qbuf_ref.at[g], q_ref.at[g], sems.at[groups + g]),
            pltpu.make_async_copy(abuf_ref.at[g], acc_ref.at[g], sems.at[2 * groups + g]),
        )

    for g in range(groups):
        load(g).start()
    norm_rows(place_ref[1], own_ref, oth_ref, normed_ref)
    first = place_ref[0] * rows
    qf_ref[...] = features(place_ref, first, rows, BIG, -BIG)
    kf_ref[...] = features(place_ref, first, rows, 1.0, 1.0)

    def group(g, carry):
        load(g).wait()
        normed = normed_ref[...]
        ones = ones_block()
        qbuf_ref[g] = head_norm(jnp.dot(normed, wbuf_ref[g, 0], preferred_element_type=F32), ones).astype(BF)
        k_ref[...] = head_norm(jnp.dot(normed, wbuf_ref[g, 1], preferred_element_type=F32), ones).astype(BF)
        v_ref[...] = jnp.dot(normed, wbuf_ref[g, 2], preferred_element_type=F32).astype(BF)

        def emit(head, r):
            abuf_ref[g, :, head * 128 : head * 128 + 128] = r.astype(BF)

        attend_group(
            lambda lanes: qbuf_ref[g, :, lanes], lambda lanes: k_ref[:, lanes], lambda lanes: v_ref[:, lanes],
            qf_ref[...], kf_ref[...], emit,
        )
        for store in stores(g):
            store.start()
        return carry

    lax.fori_loop(0, groups, group, 0)
    for g in range(groups):
        for store in stores(g):
            store.wait()


def foreign_kernel(place_ref, own_ref, oth_ref, w_ref, q_ref, acc_ref, attn_ref, t0_ref, t1_ref, t2_ref, t3_ref, normed_ref, qf_ref, kf_ref, wbuf_ref, qbuf_ref, abuf_ref, k_ref, v_ref, sum_ref, turned_ref, sems):
    rows = own_ref.shape[0]
    half = rows // 2
    groups = wbuf_ref.shape[0]
    loads = []
    for g in range(groups):
        lanes = slice(g * GROUP, g * GROUP + GROUP)
        loads.append([
            pltpu.make_async_copy(w_ref.at[1:3, :, lanes], wbuf_ref.at[g], sems.at[g]),
            pltpu.make_async_copy(q_ref.at[g], qbuf_ref.at[g], sems.at[groups + g]),
            pltpu.make_async_copy(acc_ref.at[g], abuf_ref.at[g], sems.at[2 * groups + g]),
        ])
        for load in loads[-1]:
            load.start()
    norm_rows(place_ref[1], own_ref, oth_ref, normed_ref)
    qf_ref[...] = features(place_ref, place_ref[0] * rows, rows, BIG, -BIG)
    kf_ref[...] = features(place_ref, (1 - place_ref[0]) * rows, rows, 1.0, 1.0)
    ones = ones_block()
    near = pl.ds(pl.multiple_of(place_ref[0] * half, half), half)
    far = pl.ds(pl.multiple_of((1 - place_ref[0]) * half, half), half)
    low = lower_half(rows)
    for g in range(groups):
        for load in loads[g]:
            load.wait()
        normed = normed_ref[...]
        k_ref[...] = head_norm(jnp.dot(normed, wbuf_ref[g, 0], preferred_element_type=F32), ones).astype(BF)
        v_ref[...] = jnp.dot(normed, wbuf_ref[g, 1], preferred_element_type=F32).astype(BF)

        def emit_near(head, r):
            lanes = slice(head * 128, head * 128 + 128)
            sum_ref[:, lanes] = abuf_ref[g, :, lanes].astype(F32) + r

        def emit_far(head, r):
            lanes = slice(head * 128, head * 128 + 128)
            sum_ref[far, lanes] = sum_ref[far, lanes] + r

        attend_group(
            lambda lanes: qbuf_ref[g, :, lanes], lambda lanes: k_ref[near, lanes], lambda lanes: v_ref[near, lanes],
            qf_ref[...], kf_ref[near, :], emit_near,
        )
        attend_group(
            lambda lanes: qbuf_ref[g, far, lanes], lambda lanes: k_ref[far, lanes], lambda lanes: v_ref[far, lanes],
            qf_ref[far, :], kf_ref[far, :], emit_far,
        )
        for pair in range(2):
            even = sum_ref[:, pair * 256 : pair * 256 + 128]
            odd = sum_ref[:, pair * 256 + 128 : pair * 256 + 256]
            total = pltpu.roll(jnp.where(low, odd, even), HD, 1)
            first = g * GROUP + pair * 128
            attn = (jnp.where(low, even, odd) / total).astype(BF)
            attn_ref[:, first : first + 128] = attn
            turned_ref[first : first + 128, :] = attn.T
    for i, out in enumerate((t0_ref, t1_ref, t2_ref, t3_ref)):
        part = out.shape[0]
        out[...] = turned_ref[pl.ds(pl.multiple_of((i ^ place_ref[2]) * part, part), part), :]


def send_kernel(place_ref, attn_ref, w_ref, out_ref):
    out_ref[...] = jnp.dot(attn_ref[...], w_ref[...], preferred_element_type=F32).astype(BF)


def mixed_kernel(place_ref, attn_ref, w_ref, recv_ref, pick_ref, mixed_ref, send_ref, keep_ref):
    rows = attn_ref.shape[0]
    mixed = (jnp.dot(attn_ref[...], w_ref[...], preferred_element_type=F32) + recv_ref[...].astype(F32)).astype(BF)
    mixed_ref[...] = mixed
    row = lax.broadcasted_iota(jnp.int32, (rows, rows), 1)
    for half, out in ((0, send_ref), (1, keep_ref)):
        hot = jnp.where(pick_ref[half * rows : half * rows + rows, :] == row, 1.0, 0.0).astype(BF)
        out[...] = jnp.dot(hot, mixed, preferred_element_type=F32).astype(BF)


def call(kernel, place, grid, in_specs, out_specs, out_shape, scratch, flops, nbytes, args, alias=None, limit=VMEM_LIMIT):
    return pl.pallas_call(
        kernel,
        grid_spec=pltpu.PrefetchScalarGridSpec(
            num_scalar_prefetch=1, grid=grid, in_specs=in_specs, out_specs=out_specs, scratch_shapes=scratch
        ),
        out_shape=out_shape,
        input_output_aliases=alias or {},
        cost_estimate=pl.CostEstimate(flops=flops, bytes_accessed=nbytes, transcendentals=0),
        compiler_params=pltpu.CompilerParams(vmem_limit_bytes=limit),
    )(place, *args)


def whole(shape):
    return pl.BlockSpec(shape, lambda g, s: (0,) * len(shape))


def columns(rows, width):
    return pl.BlockSpec((rows, width), lambda g, s: (0, g))


def swap(value, axis):
    return lax.ppermute(value, axis, [(0, 1), (1, 0)])


def grad_kernel(place_ref, *refs):
    lefts, rights, outs, total_ref = refs[:4], refs[4:8], refs[8:12], refs[12]
    total = jnp.dot(lefts[0][...], rights[0][...], preferred_element_type=F32)
    for left, right in zip(lefts[1:], rights[1:]):
        total = total + jnp.dot(left[...], right[...], preferred_element_type=F32)
    total_ref[...] = total
    for i, out in enumerate(outs):
        piece = out.shape[0]
        out[...] = total_ref[pl.ds(pl.multiple_of((i ^ place_ref[3]) * piece, piece), piece), :].astype(BF)


def place_kernel(place_ref, *refs, count, scale):
    out_ref = refs[-1]
    for i in range(4):
        part_ref = refs[i * count // 4]
        of_each, piece, _ = part_ref.shape
        rows = pl.ds(pl.multiple_of((i ^ place_ref[3]) * piece, piece), piece)
        out_ref[rows, :] = part_ref[i % of_each].astype(F32) * scale


AXES = ("seq", "head", "z", "y", "xl")
ROUTES = (
    (("y", 0), ("y", 1), ("z", 0), ("z", 1)),
    (("z", 0), ("z", 1), ("y", 0), ("y", 1)),
)


def across(i, kind, n):
    if kind == 0:
        return i ^ 1
    return (i + 1) % n if i % 2 else (i - 1) % n


def bit_of(i, kind):
    return ((i + 1) >> 1) & 1 if kind == 0 else (i >> 1) & 1


def every_device(sizes):
    for i in range(sizes[0] * sizes[1] * sizes[2] * sizes[3] * sizes[4]):
        at, rest = {}, i
        for name, n in reversed(list(zip(AXES, sizes))):
            at[name] = rest % n
            rest //= n
        yield i, at


def index_of(at, sizes):
    i = 0
    for name, n in zip(AXES, sizes):
        i = i * n + at[name]
    return i


def pairs(sizes, partner):
    out = []
    for i, at in every_device(sizes):
        out.append((i, index_of(partner(at), sizes)))
    return out


def quad_tables(sizes, group):
    n = dict(zip(AXES, sizes))

    def partner(at, steps):
        for step in steps:
            axis, kind = ROUTES[at["head"]][2 * group + step]
            at = {**at, axis: across(at[axis], kind, n[axis])}
        return at

    return [pairs(sizes, lambda at, steps=steps: partner(at, steps)) for steps in ((1,), (0,), (0, 1))]


def x_tables(sizes):
    n = dict(zip(AXES, sizes))

    def partner(at, kinds):
        x = at["seq"] * n["xl"] + at["xl"]
        for kind in kinds:
            x = across(x, kind, n["seq"] * n["xl"])
        return {**at, "seq": x // n["xl"], "xl": x % n["xl"]}

    return [pairs(sizes, lambda at, kinds=kinds: partner(at, kinds)) for kinds in ((0,), (1,), (0, 1))]


def z_table(sizes):
    n = sizes[AXES.index("z")]
    return pairs(sizes, lambda at: {**at, "z": (at["z"] + n // 2) % n})


def mask_of(group, head):
    masks = []
    for core in (0, 1):
        mask = jnp.int32(0)
        for axis, kind in ROUTES[core][2 * group : 2 * group + 2]:
            mask = mask * 2 + bit_of(lax.axis_index(axis).astype(jnp.int32), kind)
        masks.append(mask)
    return jnp.where(head == 0, masks[0], masks[1])


def add(*terms):
    terms = [t.astype(F32) for t in terms]
    while len(terms) > 1:
        terms = [sum(terms[i + 1 : i + 2], terms[i]) for i in range(0, len(terms), 2)]
    return terms[0].astype(BF)


def move(value, table):
    return lax.ppermute(value, AXES, table)


def place_call(place, at, scale, parts, before):
    _, piece, width = parts[0].shape
    args, specs, alias = list(parts), [whole(part.shape) for part in parts], None
    if before is not None:
        args, specs, alias = args + [before], specs + [pl.BlockSpec(memory_space=pl.ANY)], {1 + len(parts): 0}
    return call(
        functools.partial(place_kernel, count=len(parts), scale=scale), place, (1,), specs,
        pl.BlockSpec((4 * piece, width), lambda g, s: (at ^ s[2], 0)),
        jax.ShapeDtypeStruct((16 * piece, width), F32), [], 10**6, 2 * 10**6, args, alias,
    )


def grad_call(place, lefts, rights):
    part, rows = lefts[0].shape
    width = rights[0].shape[1]
    piece = part // 4
    return call(
        grad_kernel, place, (width // GROUP,),
        [whole(lefts[0].shape)] * 4 + [columns(rows, GROUP)] * 4, [columns(piece, GROUP)] * 4,
        [jax.ShapeDtypeStruct((piece, width), BF)] * 4, [pltpu.VMEM((part, GROUP), F32)],
        12 * 10**8, 8 * 10**6, (*lefts, *rights), limit=BIG_VMEM,
    )


def body(tokens, lengths, owner_slot, latent_index, cotangent, qkv_weight, out_weight):
    own = tokens[0]
    rows, share = own.shape
    groups = share // GROUP
    seq = lax.axis_index("seq")
    head = lax.axis_index("head")
    sizes = lengths[0]
    place = jnp.concatenate([jnp.stack([seq, head, mask_of(0, head), mask_of(1, head)]).astype(jnp.int32), sizes])

    oth = swap(own, "head")
    foreign_own = swap(own, "seq")
    devices = tuple(lax.axis_size(a) for a in AXES)
    first, second = quad_tables(devices, 0), quad_tables(devices, 1)
    cots = [cotangent[0]] + [move(cotangent[0], table) for table in first]

    anywhere = pl.BlockSpec(memory_space=pl.ANY)
    scratch = lambda projections: [
        pltpu.VMEM((rows, 2 * share), BF),
        pltpu.VMEM((rows, 128), BF),
        pltpu.VMEM((rows, 128), BF),
        pltpu.VMEM((groups, projections, 2 * share, GROUP), BF),
        pltpu.VMEM((groups, rows, GROUP), BF),
        pltpu.VMEM((groups, rows, 2 * GROUP), BF),
        pltpu.VMEM((rows, GROUP), BF),
        pltpu.VMEM((rows, GROUP), BF),
    ]
    q, acc = call(
        local_kernel, place, (1,), [whole((rows, share)), whole((rows, share)), anywhere], [anywhere] * 2,
        [jax.ShapeDtypeStruct((groups, rows, GROUP), BF), jax.ShapeDtypeStruct((groups, rows, 2 * GROUP), BF)],
        scratch(3) + [pltpu.SemaphoreType.DMA((3 * groups,))], 10**8, 10**6, (own, oth, qkv_weight), limit=BIG_VMEM,
    )
    foreign_own, q, cots[1], cots[2] = lax.optimization_barrier((foreign_own, q, cots[1], cots[2]))
    foreign_oth = swap(foreign_own, "head")
    quarter = whole((share // 4, rows))
    attn, *turned = call(
        foreign_kernel, place, (1,), [whole((rows, share)), whole((rows, share))] + [anywhere] * 3,
        [whole((rows, share))] + [quarter] * 4,
        [jax.ShapeDtypeStruct((rows, share), BF)] + [jax.ShapeDtypeStruct((share // 4, rows), BF)] * 4,
        scratch(2)
        + [pltpu.VMEM((rows, 2 * GROUP), F32), pltpu.VMEM((share, rows), BF), pltpu.SemaphoreType.DMA((3 * groups,))],
        10**9, 10**6, (foreign_own, foreign_oth, qkv_weight, q, acc), limit=BIG_VMEM,
    )
    attn, latent_index, sizes, owner_slot = lax.optimization_barrier((attn, latent_index, sizes, owner_slot))
    ends = jnp.cumsum(sizes, dtype=jnp.int32)
    starts = ends - sizes
    slots = owner_slot[0]
    picks = starts[:, None] + jnp.remainder(latent_index[0], sizes[:, None])
    order = slots[None, :] == jnp.arange(IMAGES, dtype=jnp.int32)[:, None]
    by_slot = jnp.sum(jnp.where(order[:, :, None], picks[None], 0), axis=1).reshape(2, rows)
    local = by_slot - seq * rows
    local = jnp.stack([jnp.where(seq == 0, local[1], local[0]), jnp.where(seq == 0, local[0], local[1])])
    local = local.reshape(2 * rows, 1)

    lefts = [turned[0]] + [move(t, table) for t, table in zip(turned[1:], first)]

    pieces = list(grad_call(place, lefts, cots))
    pieces[0], attn = lax.optimization_barrier((pieces[0], attn))
    away = [move(p, table) for p, table in zip(pieces[1:], second)]
    partial = call(
        send_kernel, place, (groups,),
        [whole((rows, share)), pl.BlockSpec((share, GROUP), lambda g, s: (0, (1 - s[1]) * groups + g))],
        columns(rows, GROUP), jax.ShapeDtypeStruct((rows, share), BF), [], 6 * 10**8, 3 * 10**6, (attn, out_weight), limit=BIG_VMEM,
    )
    away[2], partial = lax.optimization_barrier((away[2], partial))
    grad = add(pieces[0], *away)
    recv = swap(partial, "head")
    over_x = [move(grad, table) for table in x_tables(devices)]
    over_x[2], local = lax.optimization_barrier((over_x[2], local))
    grad, attn = lax.optimization_barrier((add(grad, *over_x), attn))
    over_z = move(grad, z_table(devices))
    shape = jax.ShapeDtypeStruct((rows, share), BF)
    mixed, send, keep = call(
        mixed_kernel, place, (groups,),
        [whole((rows, share)), pl.BlockSpec((share, GROUP), lambda g, s: (0, s[1] * groups + g)),
         columns(rows, GROUP), whole((2 * rows, 1))],
        [columns(rows, GROUP)] * 3, [shape] * 3, [], 14 * 10**8, 6 * 10**6, (attn, out_weight, recv, local),
    )
    over_z, send = lax.optimization_barrier((over_z, send))
    grad = add(grad, over_z)
    latents = keep + swap(send, "seq")
    held = jnp.stack([grad] + [move(grad, table) for table in second])
    across_one, across_zero = move(held, first[0]), move(held, first[1])
    scale = (2 * rows * lax.axis_size("z") * lax.axis_size("y") * lax.axis_size("xl")) ** (-0.5)
    grad_out = place_call(place, 0, scale, [held], None)
    across_one, grad_out = lax.optimization_barrier((across_one, grad_out))
    fourth = [move(across_one[:2], first[1]), move(across_zero[2:], first[0])]
    grad_out = place_call(place, 1, scale, [across_one], grad_out)
    grad_out = place_call(place, 2, scale, [across_zero], grad_out)
    grad_out = place_call(place, 3, scale, fourth, grad_out)
    return mixed[None], latents[None], grad_out


def on_mesh(fine):
    dp = ("z", "y", "xl")
    in_specs = (
        P(dp, "seq", "head"),
        P(dp, None),
        P(dp, None),
        P(dp, None, None),
        P(dp, "seq", None),
        P(None, None, "head"),
        P("head", None),
    )
    out_specs = (P(dp, "seq", "head"), P(dp, "seq", "head"), P("head", None))
    return jax.shard_map(body, mesh=fine, in_specs=in_specs, out_specs=out_specs, check_vma=False)


def solution(mesh):
    return on_mesh(Mesh(mesh.devices.reshape(2, 2, 8, 4, 2), ("seq", "head", "z", "y", "xl")))
```

```python
import functools

import jax
import jax.numpy as jnp
from jax import lax
from jax.experimental import pallas as pl
from jax.experimental.pallas import tpu as pltpu
from jax.sharding import Mesh
from jax.sharding import PartitionSpec as P

HD = 64
LAT = 128
IMAGES = 8
HEADER = 4
GROUP = 256
BIG = 128.0
EPS_NORM = 1e-05
EPS_HEAD = 1e-06
BF = jnp.bfloat16
F32 = jnp.float32
VMEM_LIMIT = 20 * 1024 * 1024
BIG_VMEM = 60 * 1024 * 1024


def norm_rows(head, own_ref, oth_ref, normed_ref):
    rows, share = own_ref.shape
    step = 128
    one = jnp.ones((share, 128), BF)
    row_sum = lambda a, b: jnp.dot(a, one, preferred_element_type=F32) + jnp.dot(b, one, preferred_element_type=F32)
    wide = lambda value: jnp.concatenate([value] * (share // 128), axis=1)
    own_at = pl.ds(pl.multiple_of(head * share, share), share)
    oth_at = pl.ds(pl.multiple_of((1 - head) * share, share), share)
    def block(i, carry):
        at = pl.ds(pl.multiple_of(i * step, step), step)
        mean = wide(row_sum(own_ref[at, :], oth_ref[at, :]) * (0.5 / share))
        own = own_ref[at, :].astype(F32) - mean
        oth = oth_ref[at, :].astype(F32) - mean
        var = row_sum((own * own).astype(BF), (oth * oth).astype(BF)) * (0.5 / share)
        scale = wide(lax.rsqrt(var + EPS_NORM))
        normed_ref[at, own_at] = (own * scale).astype(BF)
        normed_ref[at, oth_at] = (oth * scale).astype(BF)
        return carry

    lax.fori_loop(0, rows // step, block, 0)


def head_norm(values, ones):
    mean = jnp.dot((values * values).astype(BF), ones, preferred_element_type=F32)
    return values * lax.rsqrt(mean + EPS_HEAD)


def ones_block():
    row = lax.broadcasted_iota(jnp.int32, (GROUP, GROUP), 0) >> 6
    col = lax.broadcasted_iota(jnp.int32, (GROUP, GROUP), 1) >> 6
    return jnp.where(row == col, 1.0 / HD, 0.0).astype(BF)


def features(place_ref, first, rows, inside, constant):
    pos = first + lax.broadcasted_iota(jnp.int32, (rows, 128), 0)
    lane = lax.broadcasted_iota(jnp.int32, (1, 128), 1) & (HD - 1)
    starts = jnp.zeros((1, 128), jnp.int32)
    ends = jnp.zeros((1, 128), jnp.int32)
    end = jnp.int32(0)
    for i in range(IMAGES):
        starts = jnp.where(lane == i, end, starts)
        end = end + place_ref[HEADER + i]
        ends = jnp.where(lane == i, end, ends)
    member = (pos >= starts) & (pos < ends)
    return jnp.where(lane == IMAGES, constant, jnp.where(member, inside, 0.0)).astype(BF)


def lower_half(rows):
    return lax.broadcasted_iota(jnp.int32, (rows, 128), 1) < HD


def attend_group(q, k, v, qfeat, kfeat, emit):
    for pair in range(2):
        lanes = slice(pair * 128, pair * 128 + 128)
        qp, kp, vp = (q(lanes).astype(F32) * 0.125).astype(BF), k(lanes), v(lanes)
        qlow, klow = lower_half(qp.shape[0]), lower_half(kp.shape[0])
        one = jnp.ones_like(vp)
        for odd in range(2):
            qa = jnp.where(qlow, qfeat, qp) if odd else jnp.where(qlow, qp, qfeat)
            ka = jnp.where(klow, kfeat, kp) if odd else jnp.where(klow, kp, kfeat)
            va = jnp.where(klow, one, vp) if odd else jnp.where(klow, vp, one)
            s = lax.dot_general(qa, ka, (((1,), (1,)), ((), ())), preferred_element_type=F32)
            w = jnp.exp(s).astype(BF)
            emit(2 * pair + odd, jnp.dot(w, va, preferred_element_type=F32))


def local_kernel(place_ref, own_ref, oth_ref, w_ref, q_ref, acc_ref, normed_ref, qf_ref, kf_ref, wbuf_ref, qbuf_ref, abuf_ref, k_ref, v_ref, sems):
    rows = own_ref.shape[0]
    groups = wbuf_ref.shape[0]

    def load(g):
        lanes = pl.ds(pl.multiple_of(g * GROUP, GROUP), GROUP)
        return pltpu.make_async_copy(w_ref.at[:, :, lanes], wbuf_ref.at[g], sems.at[g])

    def stores(g):
        return (
            pltpu.make_async_copy(qbuf_ref.at[g], q_ref.at[g], sems.at[groups + g]),
            pltpu.make_async_copy(abuf_ref.at[g], acc_ref.at[g], sems.at[2 * groups + g]),
        )

    for g in range(groups):
        load(g).start()
    norm_rows(place_ref[1], own_ref, oth_ref, normed_ref)
    first = place_ref[0] * rows
    qf_ref[...] = features(place_ref, first, rows, BIG, -BIG)
    kf_ref[...] = features(place_ref, first, rows, 1.0, 1.0)

    def group(g, carry):
        load(g).wait()
        normed = normed_ref[...]
        ones = ones_block()
        qbuf_ref[g] = head_norm(jnp.dot(normed, wbuf_ref[g, 0], preferred_element_type=F32), ones).astype(BF)
        k_ref[...] = head_norm(jnp.dot(normed, wbuf_ref[g, 1], preferred_element_type=F32), ones).astype(BF)
        v_ref[...] = jnp.dot(normed, wbuf_ref[g, 2], preferred_element_type=F32).astype(BF)

        def emit(head, r):
            abuf_ref[g, :, head * 128 : head * 128 + 128] = r.astype(BF)

        attend_group(
            lambda lanes: qbuf_ref[g, :, lanes], lambda lanes: k_ref[:, lanes], lambda lanes: v_ref[:, lanes],
            qf_ref[...], kf_ref[...], emit,
        )
        for store in stores(g):
            store.start()
        return carry

    lax.fori_loop(0, groups, group, 0)
    for g in range(groups):
        for store in stores(g):
            store.wait()


def foreign_kernel(place_ref, own_ref, oth_ref, w_ref, q_ref, acc_ref, attn_ref, t0_ref, t1_ref, t2_ref, t3_ref, normed_ref, qf_ref, kf_ref, wbuf_ref, qbuf_ref, abuf_ref, k_ref, v_ref, sum_ref, turned_ref, sems):
    rows = own_ref.shape[0]
    half = rows // 2
    groups = wbuf_ref.shape[0]
    loads = []
    for g in range(groups):
        lanes = slice(g * GROUP, g * GROUP + GROUP)
        loads.append([
            pltpu.make_async_copy(w_ref.at[1:3, :, lanes], wbuf_ref.at[g], sems.at[g]),
            pltpu.make_async_copy(q_ref.at[g], qbuf_ref.at[g], sems.at[groups + g]),
            pltpu.make_async_copy(acc_ref.at[g], abuf_ref.at[g], sems.at[2 * groups + g]),
        ])
        for load in loads[-1]:
            load.start()
    norm_rows(place_ref[1], own_ref, oth_ref, normed_ref)
    qf_ref[...] = features(place_ref, place_ref[0] * rows, rows, BIG, -BIG)
    kf_ref[...] = features(place_ref, (1 - place_ref[0]) * rows, rows, 1.0, 1.0)
    ones = ones_block()
    near = pl.ds(pl.multiple_of(place_ref[0] * half, half), half)
    far = pl.ds(pl.multiple_of((1 - place_ref[0]) * half, half), half)
    low = lower_half(rows)
    for g in range(groups):
        for load in loads[g]:
            load.wait()
        normed = normed_ref[...]
        k_ref[...] = head_norm(jnp.dot(normed, wbuf_ref[g, 0], preferred_element_type=F32), ones).astype(BF)
        v_ref[...] = jnp.dot(normed, wbuf_ref[g, 1], preferred_element_type=F32).astype(BF)

        def emit_near(head, r):
            lanes = slice(head * 128, head * 128 + 128)
            sum_ref[:, lanes] = abuf_ref[g, :, lanes].astype(F32) + r

        def emit_far(head, r):
            lanes = slice(head * 128, head * 128 + 128)
            sum_ref[far, lanes] = sum_ref[far, lanes] + r

        attend_group(
            lambda lanes: qbuf_ref[g, :, lanes], lambda lanes: k_ref[near, lanes], lambda lanes: v_ref[near, lanes],
            qf_ref[...], kf_ref[near, :], emit_near,
        )
        attend_group(
            lambda lanes: qbuf_ref[g, far, lanes], lambda lanes: k_ref[far, lanes], lambda lanes: v_ref[far, lanes],
            qf_ref[far, :], kf_ref[far, :], emit_far,
        )
        for pair in range(2):
            even = sum_ref[:, pair * 256 : pair * 256 + 128]
            odd = sum_ref[:, pair * 256 + 128 : pair * 256 + 256]
            total = pltpu.roll(jnp.where(low, odd, even), HD, 1)
            first = g * GROUP + pair * 128
            attn = (jnp.where(low, even, odd) / total).astype(BF)
            attn_ref[:, first : first + 128] = attn
            turned_ref[first : first + 128, :] = attn.T
    for i, out in enumerate((t0_ref, t1_ref, t2_ref, t3_ref)):
        part = out.shape[0]
        out[...] = turned_ref[pl.ds(pl.multiple_of((i ^ place_ref[2]) * part, part), part), :]


def send_kernel(place_ref, attn_ref, w_ref, out_ref):
    out_ref[...] = jnp.dot(attn_ref[...], w_ref[...], preferred_element_type=F32).astype(BF)


def mixed_kernel(place_ref, attn_ref, w_ref, recv_ref, pick_ref, mixed_ref, send_ref, keep_ref, hot_ref):
    rows = attn_ref.shape[0]

    @pl.when(pl.program_id(0) == 0)
    def _():
        row = lax.broadcasted_iota(jnp.int32, (rows, rows), 0)
        for half in range(2):
            hot_ref[half] = jnp.where(pick_ref[half : half + 1, :] == row, 1.0, 0.0).astype(BF).T

    mixed = (jnp.dot(attn_ref[...], w_ref[...], preferred_element_type=F32) + recv_ref[...].astype(F32)).astype(BF)
    mixed_ref[...] = mixed
    for half, out in ((0, send_ref), (1, keep_ref)):
        out[...] = jnp.dot(hot_ref[half], mixed, preferred_element_type=F32).astype(BF)


def call(kernel, place, grid, in_specs, out_specs, out_shape, scratch, flops, nbytes, args, alias=None, limit=VMEM_LIMIT):
    return pl.pallas_call(
        kernel,
        grid_spec=pltpu.PrefetchScalarGridSpec(
            num_scalar_prefetch=1, grid=grid, in_specs=in_specs, out_specs=out_specs, scratch_shapes=scratch
        ),
        out_shape=out_shape,
        input_output_aliases=alias or {},
        cost_estimate=pl.CostEstimate(flops=flops, bytes_accessed=nbytes, transcendentals=0),
        compiler_params=pltpu.CompilerParams(vmem_limit_bytes=limit),
    )(place, *args)


def whole(shape):
    return pl.BlockSpec(shape, lambda g, s: (0,) * len(shape))


def columns(rows, width):
    return pl.BlockSpec((rows, width), lambda g, s: (0, g))


def swap(value, axis):
    return lax.ppermute(value, axis, [(0, 1), (1, 0)])


def grad_kernel(place_ref, *refs):
    lefts, rights, outs, total_ref = refs[:4], refs[4:8], refs[8:12], refs[12]
    total = jnp.dot(lefts[0][...], rights[0][...], preferred_element_type=F32)
    for left, right in zip(lefts[1:], rights[1:]):
        total = total + jnp.dot(left[...], right[...], preferred_element_type=F32)
    total_ref[...] = total
    for i, out in enumerate(outs):
        piece = out.shape[0]
        out[...] = total_ref[pl.ds(pl.multiple_of((i ^ place_ref[3]) * piece, piece), piece), :].astype(BF)


def place_kernel(place_ref, *refs, count, scale):
    out_ref = refs[-1]
    for i in range(4):
        part_ref = refs[i * count // 4]
        of_each, piece, _ = part_ref.shape
        rows = pl.ds(pl.multiple_of((i ^ place_ref[3]) * piece, piece), piece)
        out_ref[rows, :] = part_ref[i % of_each].astype(F32) * scale


AXES = ("seq", "head", "z", "y", "xl")
ROUTES = (
    (("y", 0), ("y", 1), ("z", 0), ("z", 1)),
    (("z", 0), ("z", 1), ("y", 0), ("y", 1)),
)


def across(i, kind, n):
    if kind == 0:
        return i ^ 1
    return (i + 1) % n if i % 2 else (i - 1) % n


def bit_of(i, kind):
    return ((i + 1) >> 1) & 1 if kind == 0 else (i >> 1) & 1


def every_device(sizes):
    for i in range(sizes[0] * sizes[1] * sizes[2] * sizes[3] * sizes[4]):
        at, rest = {}, i
        for name, n in reversed(list(zip(AXES, sizes))):
            at[name] = rest % n
            rest //= n
        yield i, at


def index_of(at, sizes):
    i = 0
    for name, n in zip(AXES, sizes):
        i = i * n + at[name]
    return i


def pairs(sizes, partner):
    out = []
    for i, at in every_device(sizes):
        out.append((i, index_of(partner(at), sizes)))
    return out


def quad_tables(sizes, group):
    n = dict(zip(AXES, sizes))

    def partner(at, steps):
        for step in steps:
            axis, kind = ROUTES[at["head"]][2 * group + step]
            at = {**at, axis: across(at[axis], kind, n[axis])}
        return at

    return [pairs(sizes, lambda at, steps=steps: partner(at, steps)) for steps in ((1,), (0,), (0, 1))]


def x_tables(sizes):
    n = dict(zip(AXES, sizes))

    def partner(at, kinds):
        x = at["seq"] * n["xl"] + at["xl"]
        for kind in kinds:
            x = across(x, kind, n["seq"] * n["xl"])
        return {**at, "seq": x // n["xl"], "xl": x % n["xl"]}

    return [pairs(sizes, lambda at, kinds=kinds: partner(at, kinds)) for kinds in ((0,), (1,), (0, 1))]


def z_table(sizes):
    n = sizes[AXES.index("z")]
    return pairs(sizes, lambda at: {**at, "z": (at["z"] + n // 2) % n})


def mask_of(group, head):
    masks = []
    for core in (0, 1):
        mask = jnp.int32(0)
        for axis, kind in ROUTES[core][2 * group : 2 * group + 2]:
            mask = mask * 2 + bit_of(lax.axis_index(axis).astype(jnp.int32), kind)
        masks.append(mask)
    return jnp.where(head == 0, masks[0], masks[1])


def add(*terms):
    terms = [t.astype(F32) for t in terms]
    while len(terms) > 1:
        terms = [sum(terms[i + 1 : i + 2], terms[i]) for i in range(0, len(terms), 2)]
    return terms[0].astype(BF)


def move(value, table):
    return lax.ppermute(value, AXES, table)


def place_call(place, at, scale, parts, before):
    _, piece, width = parts[0].shape
    args, specs, alias = list(parts), [whole(part.shape) for part in parts], None
    if before is not None:
        args, specs, alias = args + [before], specs + [pl.BlockSpec(memory_space=pl.ANY)], {1 + len(parts): 0}
    return call(
        functools.partial(place_kernel, count=len(parts), scale=scale), place, (1,), specs,
        pl.BlockSpec((4 * piece, width), lambda g, s: (at ^ s[2], 0)),
        jax.ShapeDtypeStruct((16 * piece, width), F32), [], 10**6, 2 * 10**6, args, alias,
    )


def grad_call(place, lefts, rights):
    part, rows = lefts[0].shape
    width = rights[0].shape[1]
    piece = part // 4
    return call(
        grad_kernel, place, (width // (2 * GROUP),),
        [whole(lefts[0].shape)] * 4 + [columns(rows, 2 * GROUP)] * 4, [columns(piece, 2 * GROUP)] * 4,
        [jax.ShapeDtypeStruct((piece, width), BF)] * 4, [pltpu.VMEM((part, 2 * GROUP), F32)],
        12 * 10**8, 8 * 10**6, (*lefts, *rights), limit=BIG_VMEM,
    )


def body(tokens, lengths, owner_slot, latent_index, cotangent, qkv_weight, out_weight):
    own = tokens[0]
    rows, share = own.shape
    groups = share // GROUP
    seq = lax.axis_index("seq")
    head = lax.axis_index("head")
    sizes = lengths[0]
    place = jnp.concatenate([jnp.stack([seq, head, mask_of(0, head), mask_of(1, head)]).astype(jnp.int32), sizes])

    oth = swap(own, "head")
    foreign_own = swap(own, "seq")
    devices = tuple(lax.axis_size(a) for a in AXES)
    first, second = quad_tables(devices, 0), quad_tables(devices, 1)
    cots = [cotangent[0]] + [move(cotangent[0], table) for table in first]

    anywhere = pl.BlockSpec(memory_space=pl.ANY)
    scratch = lambda projections: [
        pltpu.VMEM((rows, 2 * share), BF),
        pltpu.VMEM((rows, 128), BF),
        pltpu.VMEM((rows, 128), BF),
        pltpu.VMEM((groups, projections, 2 * share, GROUP), BF),
        pltpu.VMEM((groups, rows, GROUP), BF),
        pltpu.VMEM((groups, rows, 2 * GROUP), BF),
        pltpu.VMEM((rows, GROUP), BF),
        pltpu.VMEM((rows, GROUP), BF),
    ]
    q, acc = call(
        local_kernel, place, (1,), [whole((rows, share)), whole((rows, share)), anywhere], [anywhere] * 2,
        [jax.ShapeDtypeStruct((groups, rows, GROUP), BF), jax.ShapeDtypeStruct((groups, rows, 2 * GROUP), BF)],
        scratch(3) + [pltpu.SemaphoreType.DMA((3 * groups,))], 10**8, 10**6, (own, oth, qkv_weight), limit=BIG_VMEM,
    )
    foreign_own, q, cots[1], cots[2] = lax.optimization_barrier((foreign_own, q, cots[1], cots[2]))
    foreign_oth = swap(foreign_own, "head")
    quarter = whole((share // 4, rows))
    attn, *turned = call(
        foreign_kernel, place, (1,), [whole((rows, share)), whole((rows, share))] + [anywhere] * 3,
        [whole((rows, share))] + [quarter] * 4,
        [jax.ShapeDtypeStruct((rows, share), BF)] + [jax.ShapeDtypeStruct((share // 4, rows), BF)] * 4,
        scratch(2)
        + [pltpu.VMEM((rows, 2 * GROUP), F32), pltpu.VMEM((share, rows), BF), pltpu.SemaphoreType.DMA((3 * groups,))],
        10**9, 10**6, (foreign_own, foreign_oth, qkv_weight, q, acc), limit=BIG_VMEM,
    )
    attn, latent_index, sizes, owner_slot = lax.optimization_barrier((attn, latent_index, sizes, owner_slot))
    ends = jnp.cumsum(sizes, dtype=jnp.int32)
    starts = ends - sizes
    slots = owner_slot[0]
    picks = starts[:, None] + jnp.remainder(latent_index[0], sizes[:, None])
    order = slots[None, :] == jnp.arange(IMAGES, dtype=jnp.int32)[:, None]
    by_slot = jnp.sum(jnp.where(order[:, :, None], picks[None], 0), axis=1).reshape(2, rows)
    local = by_slot - seq * rows
    local = jnp.stack([jnp.where(seq == 0, local[1], local[0]), jnp.where(seq == 0, local[0], local[1])])

    lefts = [turned[0]] + [move(t, table) for t, table in zip(turned[1:], first)]

    pieces = list(grad_call(place, lefts, cots))
    pieces[0], attn = lax.optimization_barrier((pieces[0], attn))
    away = [move(p, table) for p, table in zip(pieces[1:], second)]
    partial = call(
        send_kernel, place, (groups,),
        [whole((rows, share)), pl.BlockSpec((share, GROUP), lambda g, s: (0, (1 - s[1]) * groups + g))],
        columns(rows, GROUP), jax.ShapeDtypeStruct((rows, share), BF), [], 6 * 10**8, 3 * 10**6, (attn, out_weight), limit=BIG_VMEM,
    )
    away[2], partial = lax.optimization_barrier((away[2], partial))
    grad = add(pieces[0], *away)
    recv = swap(partial, "head")
    over_x = [move(grad, table) for table in x_tables(devices)]
    over_x[2], local = lax.optimization_barrier((over_x[2], local))
    grad, attn = lax.optimization_barrier((add(grad, *over_x), attn))
    over_z = move(grad, z_table(devices))
    shape = jax.ShapeDtypeStruct((rows, share), BF)
    mixed, send, keep = call(
        mixed_kernel, place, (groups,),
        [whole((rows, share)), pl.BlockSpec((share, GROUP), lambda g, s: (0, s[1] * groups + g)),
         columns(rows, GROUP), whole((2, rows))],
        [columns(rows, GROUP)] * 3, [shape] * 3, [pltpu.VMEM((2, rows, rows), BF)], 14 * 10**8, 6 * 10**6, (attn, out_weight, recv, local),
    )
    over_z, send = lax.optimization_barrier((over_z, send))
    grad = add(grad, over_z)
    latents = keep + swap(send, "seq")
    held = jnp.stack([grad] + [move(grad, table) for table in second])
    across_one, across_zero = move(held, first[0]), move(held, first[1])
    scale = (2 * rows * lax.axis_size("z") * lax.axis_size("y") * lax.axis_size("xl")) ** (-0.5)
    grad_out = place_call(place, 0, scale, [held], None)
    across_one, grad_out = lax.optimization_barrier((across_one, grad_out))
    fourth = [move(across_one[:2], first[1]), move(across_zero[2:], first[0])]
    grad_out = place_call(place, 1, scale, [across_one], grad_out)
    grad_out = place_call(place, 2, scale, [across_zero], grad_out)
    grad_out = place_call(place, 3, scale, fourth, grad_out)
    return mixed[None], latents[None], grad_out


def on_mesh(fine):
    dp = ("z", "y", "xl")
    in_specs = (
        P(dp, "seq", "head"),
        P(dp, None),
        P(dp, None),
        P(dp, None, None),
        P(dp, "seq", None),
        P(None, None, "head"),
        P("head", None),
    )
    out_specs = (P(dp, "seq", "head"), P(dp, "seq", "head"), P("head", None))
    return jax.shard_map(body, mesh=fine, in_specs=in_specs, out_specs=out_specs, check_vma=False)


def solution(mesh):
    return on_mesh(Mesh(mesh.devices.reshape(2, 2, 8, 4, 2), ("seq", "head", "z", "y", "xl")))
```
